128 devices in a mesh: flow: 32 (over x, y, core), mech: 4 (over z).
Axes of the slice: x: 4, y: 4, z: 4, core: 2. Of those that a mesh axis runs over, the one named last changes fastest.
Arguments:
- source: float32 [2048, 128], P('flow'), may hold values from -6 to 6
- aperture_rest: float32 [2048, 128], P('flow'), may hold values from 0.5 to 2
- storage: float32 [2048, 128], P('flow'), may hold values from 0.5 to 2
- geometry: float32 [2048, 128], P('flow'), may hold values from 0.2 to 1
- tiles: float32 [2048, 128, 128], P('flow'), as said below
- near: bfloat16 [512, 512, 512], P('flow', None, 'mech'), may hold values from -0.25 to 0.25
- basis_in: float32 [262144, 64], P('flow'), may hold values from -0.01171875 to 0.01171875
- core: float32 [64, 64], replicated, may hold values from -0.75 to 0.75
- basis_out: float32 [262144, 64], P('flow'), may hold values from -0.75 to 0.75
Outputs:
- pressure: float32 [2048, 128], P('flow')
- aperture: float32 [2048, 128], P('flow')
The draws below stay inside these ranges and needn't reach their ends.
Inputs may be any that keep to these rules, and one draw needn't show every extreme that they name: `tiles`: each tile is symmetric with its eigenvalues between 1 and 4.
All inputs are finite; a program needn't handle non-finite values.
Results may differ from the reference program's by a relative error of at most 0.00033.
Values sent between devices are 32-bit elements; how exact they have to be, the bound alone decides.
A program may use at most 64 MiB of HBM per device.

```python
import math
import jax
import jax.numpy as jnp
from jax import lax

B = 128
RANK = 64
CG = 5
COUPLE = 1
NBT = 2048
NELEM = 262144
CL = 512
NCT = 512


def draw_tiles(key, part):
    key = jax.random.fold_in(key, 11)
    key_off, key_diag = jax.random.split(key)
    raw = jax.random.normal(key_off, (NBT, B, B), jnp.float32)
    raw = jnp.clip(raw, -4.0, 4.0)
    offdiag = (raw + jnp.swapaxes(raw, 1, 2)) * (0.35 / (2.0 * B) ** 0.5)
    rows = jnp.arange(B)[:, None]
    cols = jnp.arange(B)[None, :]
    eye = (rows == cols).astype(jnp.float32)
    offdiag = offdiag * (1.0 - eye)[None]
    diag = 2.0 + jax.random.uniform(key_diag, (NBT, B), jnp.float32)
    return offdiag + eye[None] * diag[:, :, None]


def block_levels(stream_key, dims, pieces, smallest, largest):
    loudness, own = 1.0, jax.random.fold_in(stream_key, 6)
    for axis_at, shards_of in pieces:
        heights = jnp.exp(jax.random.uniform(jax.random.fold_in(own, axis_at), (shards_of,), jnp.float32, smallest / len(pieces), largest / len(pieces)))
        loudness = loudness * jnp.repeat(heights, dims[axis_at] // shards_of).reshape([-1 if axis == axis_at else 1 for axis in range(len(dims))])
    return loudness


def normal_values(own_key, shape, spread, limit, cuts=(), dtype=jnp.bfloat16):
    gain = block_levels(own_key, shape, cuts, -0.22, 0.18) if cuts else 1.0
    values = jax.random.normal(own_key, shape, jnp.float32) * spread * gain
    return jnp.minimum(jnp.maximum(values, -limit), limit).astype(dtype)


def setup_inputs(seed: int = 0) -> dict:
    splits = jax.random.split(jax.random.key(seed), 10)
    source = normal_values(splits[0], (NBT, B), 1.0, 6.0, ((0, 32),), jnp.float32)
    aperture_rest = jnp.clip(jnp.exp(math.log(2.0) - 1.3862944 * jax.random.uniform(splits[1], (NBT, B), jnp.float32) ** block_levels(splits[1], (NBT, B), ((0, 32),), -0.2, 0.2)), 0.5, 2.0)
    storage = jnp.clip(jnp.exp(math.log(2.0) - 1.3862944 * jax.random.uniform(splits[2], (NBT, B), jnp.float32) ** block_levels(splits[2], (NBT, B), ((0, 32),), -0.2, 0.2)), 0.5, 2.0)
    geometry = jnp.clip(jnp.exp(math.log(1.0) - 1.609438 * jax.random.uniform(splits[3], (NBT, B), jnp.float32) ** block_levels(splits[3], (NBT, B), ((0, 32),), -0.2, 0.2)), 0.2, 1.0)
    tiles = draw_tiles(jax.random.fold_in(splits[9], 71), 0)
    near = normal_values(splits[5], (NCT, CL, CL), CL ** -0.5, 0.25, ((0, 32), (2, 4)))
    basis_in = normal_values(splits[6], (NELEM, RANK), NELEM ** -0.5, 0.01171875, ((0, 32),), jnp.float32)
    core = normal_values(splits[7], (RANK, RANK), RANK ** -0.5, 0.75, (), jnp.float32)
    basis_out = normal_values(splits[8], (NELEM, RANK), RANK ** -0.5, 0.75, ((0, 32),), jnp.float32)
    return {"source": source, "aperture_rest": aperture_rest, "storage": storage, "geometry": geometry, "tiles": tiles, "near": near, "basis_in": basis_in, "core": core, "basis_out": basis_out}


def couplings(aperture):
    zero = jnp.zeros((1, aperture.shape[1]), jnp.float32)
    nxt = jnp.concatenate([aperture[1:], zero], axis=0)
    return (aperture ** 3 + nxt ** 3) * 0.5


def operate(v, tiles, scale, storage, cond):
    zero = jnp.zeros((1, v.shape[1]), jnp.float32)
    local = jnp.einsum('bij,bj->bi', tiles, scale * v, precision=lax.Precision.HIGHEST) * scale
    nxt = jnp.concatenate([v[1:], zero], axis=0)
    prv = jnp.concatenate([zero, v[:-1]], axis=0)
    cprv = jnp.concatenate([zero, cond[:-1]], axis=0)
    return storage * v + local + (cond + cprv) * v - cond * nxt - cprv * prv


def reference(source, aperture_rest, storage, geometry, tiles, near, basis_in, core, basis_out):
    aperture = aperture_rest
    pressure = jnp.zeros_like(source)
    for outer in range(COUPLE):
        scale = aperture ** 1.5
        cond = geometry * couplings(aperture)
        pressure = jnp.zeros_like(source)
        residual = source
        direction = source
        norm_now = jnp.sum(residual * residual)
        for step in range(CG):
            image = operate(direction, tiles, scale, storage, cond)
            alpha = norm_now / jnp.sum(direction * image)
            pressure = pressure + alpha * direction
            residual = residual - alpha * image
            norm_next = jnp.sum(residual * residual)
            direction = residual + (norm_next / norm_now) * direction
            norm_now = norm_next
        packed = pressure.astype(jnp.bfloat16).reshape(NCT, CL)
        near_disp = lax.map(lambda pair: jnp.dot(pair[0], pair[1], preferred_element_type=jnp.float32), (near, packed))
        near_disp = near_disp.reshape(NBT, B)
        coeffs = jnp.dot(pressure.reshape(-1), basis_in, precision=lax.Precision.HIGHEST)
        mixed = jnp.dot(core, coeffs, precision=lax.Precision.HIGHEST)
        far_disp = jnp.dot(basis_out, mixed, precision=lax.Precision.HIGHEST).reshape(NBT, B)
        aperture = aperture_rest * (1.0 + 0.5 * jnp.tanh(near_disp + far_disp))
    return pressure, aperture
```

```python
import functools
import jax
import jax.numpy as jnp
from jax import lax
from jax.experimental import pallas as pl
from jax.experimental.pallas import tpu as pltpu
from jax.sharding import PartitionSpec as P

F32 = jnp.float32
BF16 = jnp.bfloat16
MESH = pl.DeviceIdType.MESH
NV = 5
TOP = 8


def split(x):
    hi = x.astype(BF16)
    return hi, (x - hi.astype(F32)).astype(BF16)


def tile_group(weights, u, g):
    hi, lo = split(u)
    left = jnp.concatenate(
        [jnp.concatenate([hi, hi], 1), jnp.concatenate([lo, jnp.zeros_like(lo)], 1)], 0
    )
    out = jnp.dot(left, weights[g], preferred_element_type=F32)
    rows = [
        out[k : k + 1, k * 128 : k * 128 + 128] + out[8 + k : 9 + k, k * 128 : k * 128 + 128]
        for k in range(8)
    ]
    return jnp.concatenate(rows, axis=0)


def kernel(
    nf, nm, blocks,
    src_h, ap_h, st_h, ge_h, tiles_h, near_h, bin_h, core_h, bout_h,
    p_h, a_h,
    src, ap, st, ge, tiles, weights, near, bin_v, core, bout,
    vec, img, diag, cnext, cprev, scale, p_v, a_v, far, rows,
    h0s, h0r, es, er, m1, m2, m3, mz,
    lsem, tsem, osem, h0sem, esem, bsem, zsem,
):
    me = lax.axis_index("flow")
    owner = lax.axis_index("mech")
    right = lax.rem(me + 1, nf)
    left = lax.rem(me + nf - 1, nf)
    groups = blocks // 8
    chunk = blocks // 4

    loads = []

    def load(i, a, b):
        c = pltpu.make_async_copy(a, b, lsem.at[i])
        c.start()
        loads.append(c)

    load(0, src_h, src)
    load(1, ap_h, ap)
    load(2, ge_h, ge)
    load(3, st_h, st)
    tloads = []
    for q in range(4):
        part = pl.ds(q * chunk, chunk)
        c = pltpu.make_async_copy(tiles_h.at[part], tiles.at[part], tsem.at[q])
        c.start()
        tloads.append(c)
    load(4, bin_h, bin_v)
    load(5, near_h, near)
    load(6, core_h, core)
    load(7, bout_h, bout)

    barrier = pltpu.get_barrier_semaphore()

    def greet(d, carry):
        pl.semaphore_signal(
            barrier, inc=1, device_id={"flow": lax.rem(me + d, nf)}, device_id_type=MESH
        )
        return carry

    lax.fori_loop(1, nf, greet, 0)
    for d in range(1, nm):
        pl.semaphore_signal(
            barrier, inc=1, device_id={"mech": lax.rem(owner + d, nm)}, device_id_type=MESH
        )

    for i in range(3):
        loads[i].wait()
    last = blocks - 1
    h0s[0, 0] = ap[last : last + 1, :]
    h0s[0, 1] = ge[last : last + 1, :]
    h0s[0, 2] = src[last : last + 1, :]
    h0s[1, 0] = ap[0:1, :]
    h0s[1, 1] = ge[0:1, :]
    h0s[1, 2] = src[0:1, :]
    rows[...] = jnp.zeros_like(rows)
    pl.semaphore_wait(barrier, nf - 1 + nm - 1)

    pending = []

    def shift_out(sbuf, rbuf, ssem, rsem):
        out = []
        for side, dev in ((0, right), (1, left)):
            c = pltpu.make_async_remote_copy(
                src_ref=sbuf.at[side],
                dst_ref=rbuf.at[side],
                send_sem=ssem.at[side],
                recv_sem=rsem.at[side],
                device_id={"flow": dev},
                device_id_type=MESH,
            )
            c.start()
            out.append(c)
            pending.append(c)
        return out

    def spread(buf, i):
        def one(d, carry):
            pltpu.make_async_remote_copy(
                src_ref=buf.at[me],
                dst_ref=buf.at[me],
                send_sem=bsem.at[i, 0],
                recv_sem=bsem.at[i, 1],
                device_id={"flow": lax.rem(me + d, nf)},
                device_id_type=MESH,
            ).start()
            return carry

        lax.fori_loop(1, nf, one, 0)

    def gather_wait(buf, i, which):
        others = buf.at[pl.ds(0, nf - 1)]
        pltpu.make_async_copy(others, others, bsem.at[i, which]).wait()

    first_halo = shift_out(h0s, h0r, h0sem.at[0], h0sem.at[1])

    a = ap[...]
    s = a * jnp.sqrt(a)
    scale[...] = s
    b = src[...]
    body = slice(TOP, TOP + blocks)
    above = slice(TOP - 1, TOP - 1 + blocks)
    below = slice(TOP + 1, TOP + 1 + blocks)
    for k in range(NV):
        vec[k, TOP - 1 : TOP, :] = jnp.zeros((1, 128), F32)
        vec[k, TOP + blocks : TOP + blocks + 1, :] = jnp.zeros((1, 128), F32)
    vec[0, body, :] = b

    for q in range(4):
        tloads[q].wait()
        for g in range(q * groups // 4, (q + 1) * groups // 4):
            for k in range(8):
                hi, lo = split(tiles[g * 8 + k])
                weights[g, 0:128, k * 128 : k * 128 + 128] = hi
                weights[g, 128:256, k * 128 : k * 128 + 128] = lo
            part = slice(g * 8, g * 8 + 8)
            img[0, part, :] = tile_group(weights, scale[part, :] * src[part, :], g)

    loads[3].wait()
    for c in first_halo:
        c.wait_recv()
    zero_row = jnp.zeros((1, 128), F32)
    head = me == 0
    tail = me == nf - 1
    ap_next = jnp.where(tail, zero_row, h0r[1, 0])
    cube = a * a * a
    cube_next = jnp.concatenate([cube[1:], ap_next * ap_next * ap_next], axis=0)
    cond = ge[...] * (cube + cube_next) * 0.5
    ap_prev = h0r[0, 0]
    cond_prev = h0r[0, 1] * (ap_prev * ap_prev * ap_prev + cube[0:1]) * 0.5
    cond_prev = jnp.where(head, zero_row, cond_prev)
    cp = jnp.concatenate([cond_prev, cond[:-1]], axis=0)
    cnext[...] = cond
    cprev[...] = cp
    cnext[last : last + 1, :] = jnp.where(tail, zero_row, cond[last:])
    diag[...] = st[...] + cond + cp
    vec[0, TOP - 1 : TOP, :] = h0r[0, 2]
    vec[0, TOP + blocks : TOP + blocks + 1, :] = h0r[1, 2]

    def finish(k):
        img[k] = (
            diag[...] * vec[k, body, :]
            + scale[...] * img[k]
            - cnext[...] * vec[k, below, :]
            - cprev[...] * vec[k, above, :]
        )

    def product(k):
        for g in range(groups):
            part = slice(g * 8, g * 8 + 8)
            u = scale[part, :] * vec[k, TOP + g * 8 : TOP + g * 8 + 8, :]
            img[k, part, :] = tile_group(weights, u, g)

    def send_edges(k, i):
        es[i, 0] = vec[k, TOP + last : TOP + blocks, :]
        es[i, 1] = vec[k, TOP : TOP + 1, :]
        return shift_out(es.at[i], er.at[i], esem.at[i, 0], esem.at[i, 1])

    def patch(copies, k, i):
        for c in copies:
            c.wait_recv()
        img[k, 0:1, :] = img[k, 0:1, :] - cprev[0:1, :] * er[i, 0]
        img[k, last : last + 1, :] = (
            img[k, last : last + 1, :] - cnext[last : last + 1, :] * er[i, 1]
        )

    def dot_row(i, x, y):
        rows[i : i + 1, :] = jnp.sum(x * y, axis=0, keepdims=True)

    def row_sums():
        return jnp.sum(rows[...].T, axis=0, keepdims=True)

    def lane(row, i):
        return jnp.broadcast_to(row[:, i : i + 1], (1, 128))

    finish(0)
    w0 = img[0]
    vec[1, body, :] = w0
    copies = send_edges(1, 0)
    dot_row(0, b, b)
    dot_row(1, b, w0)
    dot_row(2, w0, w0)
    m1[me] = jnp.zeros((1, 128), F32)
    m1[me, 0:1, 0:32] = row_sums()
    spread(m1, 0)
    product(1)
    finish(1)
    patch(copies, 1, 0)

    gather_wait(m1, 0, 1)
    total = jnp.sum(m1[...], axis=0)
    bb, bw, ww = lane(total, 0), lane(total, 1), lane(total, 2)
    mean = bw / bb
    dev = jnp.sqrt(jnp.maximum(ww / bb - mean * mean, (0.01 * mean) * (0.01 * mean)))
    inv = 1.0 / dev
    center = mean + 0.8 * dev
    shifted = center * inv
    w0 = img[0]
    v1 = (w0 - mean * src[...]) * inv
    w1 = (img[1] - mean * w0) * inv
    vec[1, body, :] = v1
    img[1] = w1
    vec[2, body, :] = w1 * inv - shifted * v1 - src[...]
    copies = send_edges(2, 1)
    product(2)
    finish(2)
    b = src[...]
    v2 = vec[2, body, :]
    pairs = {}

    def entry(j, k):
        pairs[(j, k)] = len(pairs)
        dot_row(pairs[(j, k)], vec[k, body, :], img[j])

    def against(k):
        pairs[("g", k)] = len(pairs)
        dot_row(pairs[("g", k)], vec[k, body, :], vec[1, body, :])

    entry(0, 0)
    entry(0, 1)
    entry(1, 1)
    entry(0, 2)
    entry(1, 2)
    against(1)
    against(2)
    patch(copies, 2, 1)
    vec[3, body, :] = img[2] * inv - shifted * v2 - vec[1, body, :]
    copies = send_edges(3, 2)
    product(3)
    finish(3)
    entry(2, 2)
    entry(0, 3)
    entry(1, 3)
    entry(2, 3)
    against(3)
    patch(copies, 3, 2)
    vec[4, body, :] = img[3] * inv - shifted * vec[3, body, :] - v2
    product(4)
    finish(4)
    entry(3, 3)
    for j in range(4):
        entry(j, 4)
    entry(4, 4)
    against(4)
    m2[me, 0] = jnp.zeros((1, 128), F32)
    m2[me, 0, 0:1, 0:32] = row_sums()
    m2[me, 1] = cnext[last : last + 1, :] * vec[4, TOP + last : TOP + blocks, :]
    m2[me, 2] = vec[4, TOP : TOP + 1, :]
    spread(m2, 1)
    loads[4].wait()
    loads[5].wait()
    gather_wait(m2, 1, 1)

    total = jnp.sum(m2[:, 0], axis=0)
    cross = jnp.sum(m2[0 : nf - 1, 1] * m2[1:nf, 2], axis=0)
    cross = jnp.broadcast_to(jnp.sum(cross, axis=1, keepdims=True), (1, 128))
    full = [[None] * NV for _ in range(NV)]
    for j in range(NV):
        for k in range(j, NV):
            full[j][k] = lane(total, pairs[(j, k)])
    full[4][4] = full[4][4] - 2.0 * cross
    size = [full[j][j] for j in range(NV)]
    ratio = -dev / mean
    y = [jnp.zeros((1, 128), F32)] + [ratio * lane(total, pairs[("g", k)]) for k in range(1, NV)]
    low = [[None] * NV for _ in range(NV)]
    pivot = [None] * NV
    for j in range(NV):
        good = full[j][j] > 1e-6 * size[j]
        pivot[j] = jnp.where(good, 1.0 / jnp.where(good, full[j][j], 1.0), 0.0)
        for i in range(j + 1, NV):
            low[i][j] = full[j][i] * pivot[j]
        for i in range(j + 1, NV):
            for k in range(i, NV):
                full[i][k] = full[i][k] - low[i][j] * full[j][k]
            y[i] = y[i] - low[i][j] * y[j]
    coef = [y[j] * pivot[j] for j in range(NV)]
    for j in range(NV - 2, -1, -1):
        for i in range(j + 1, NV):
            coef[j] = coef[j] - low[i][j] * coef[i]
    coef[0] = coef[0] + 1.0 / mean
    p = coef[0] * vec[0, body, :]
    for k in range(1, NV):
        p = p + coef[k] * vec[k, body, :]
    p_v[...] = p
    out_p = pltpu.make_async_copy(p_v, p_h, osem.at[0])
    out_p.start()

    acc = jnp.zeros((64, 128), F32)
    for g in range(blocks):
        acc = acc + bin_v[:, g * 128 : g * 128 + 128] * p_v[g : g + 1, :]
    m3[me] = jnp.zeros((1, 128), F32)
    m3[me, 0:1, 0:64] = jnp.sum(acc.T, axis=0, keepdims=True)
    spread(m3, 2)

    clusters = blocks // nm
    mine = jnp.zeros((clusters, 128), F32)
    for q in range(nm):
        mine = jnp.where(owner == q, p_v[pl.ds(q, clusters, stride=nm), :], mine)
    mine = mine.astype(BF16)
    for c in range(clusters):
        full_c = lax.dot_general(
            mine, near[c], (((1,), (1,)), ((), ())), preferred_element_type=F32
        )
        for q in range(nm):
            mz[owner, nm * c + q : nm * c + q + 1, :] = full_c[c : c + 1, q * 128 : q * 128 + 128]
    for d in range(1, nm):
        c = pltpu.make_async_remote_copy(
            src_ref=mz.at[owner],
            dst_ref=mz.at[owner],
            send_sem=zsem.at[0],
            recv_sem=zsem.at[1],
            device_id={"mech": lax.rem(owner + d, nm)},
            device_id_type=MESH,
        )
        c.start()

    loads[6].wait()
    loads[7].wait()
    gather_wait(m3, 2, 1)
    coeffs = jnp.sum(m3[...], axis=0)[:, 0:64]
    mixed = jnp.sum(core[...] * coeffs, axis=1, keepdims=True)
    mixed = jnp.broadcast_to(mixed, (64, 128))
    for g in range(blocks):
        far[g : g + 1, :] = jnp.sum(
            bout[:, g * 128 : g * 128 + 128] * mixed, axis=0, keepdims=True
        )
    others = mz.at[pl.ds(0, nm - 1)]
    pltpu.make_async_copy(others, others, zsem.at[1]).wait()
    shift = jnp.sum(mz[...], axis=0) + far[...]
    a_v[...] = ap[...] * (1.0 + 0.5 * jnp.tanh(shift))
    out_a = pltpu.make_async_copy(a_v, a_h, osem.at[1])
    out_a.start()
    for c in pending:
        c.wait_send()
    for buf, i in ((m1, 0), (m2, 1), (m3, 2)):
        gather_wait(buf, i, 0)
    pltpu.make_async_copy(others, others, zsem.at[0]).wait()
    out_p.wait()
    out_a.wait()


def solution(mesh):
    nf = mesh.shape["flow"]
    nm = mesh.shape["mech"]

    def local(source, aperture_rest, storage, geometry, tiles, near, basis_in, core, basis_out):
        blocks, width = source.shape
        rank = core.shape[0]
        grid = (blocks, width)
        vm = pltpu.VMEM
        scratch = [
            vm(grid, F32), vm(grid, F32), vm(grid, F32), vm(grid, F32),
            vm(tiles.shape, F32), vm((blocks // 8, 2 * width, 8 * width), BF16),
            vm(near.shape, BF16), vm((rank, basis_in.shape[0]), F32), vm(core.shape, F32),
            vm((rank, basis_in.shape[0]), F32),
            vm((NV, blocks + 2 * TOP, width), F32), vm((NV,) + grid, F32),
            vm(grid, F32), vm(grid, F32), vm(grid, F32), vm(grid, F32),
            vm(grid, F32), vm(grid, F32), vm(grid, F32), vm((32, width), F32),
            vm((2, 3, 1, width), F32), vm((2, 3, 1, width), F32),
            vm((3, 2, 1, width), F32), vm((3, 2, 1, width), F32),
            vm((nf, 1, width), F32), vm((nf, 3, 1, width), F32), vm((nf, 1, width), F32),
            vm((nm,) + grid, F32),
            pltpu.SemaphoreType.DMA((8,)), pltpu.SemaphoreType.DMA((4,)),
            pltpu.SemaphoreType.DMA((2,)), pltpu.SemaphoreType.DMA((2, 2)),
            pltpu.SemaphoreType.DMA((3, 2, 2)), pltpu.SemaphoreType.DMA((3, 2)),
            pltpu.SemaphoreType.DMA((2,)),
        ]
        anywhere = pl.BlockSpec(memory_space=pl.ANY)
        return pl.pallas_call(
            functools.partial(kernel, nf, nm, blocks),
            out_shape=(jax.ShapeDtypeStruct(grid, F32), jax.ShapeDtypeStruct(grid, F32)),
            in_specs=[anywhere] * 9,
            out_specs=(anywhere, anywhere),
            scratch_shapes=scratch,
            compiler_params=pltpu.CompilerParams(
                collective_id=0, has_side_effects=True, vmem_limit_bytes=48 << 20
            ),
        )(
            source, aperture_rest, storage, geometry, tiles, near,
            basis_in.T, core, basis_out.T,
        )

    placed = (
        P("flow", None), P("flow", None), P("flow", None), P("flow", None),
        P("flow", None, None), P("flow", None, "mech"), P("flow", None), P(), P("flow", None),
    )
    return jax.shard_map(
        local,
        mesh=mesh,
        in_specs=placed,
        out_specs=(P("flow", None), P("flow", None)),
        check_vma=False,
    )
```

```python
import functools
import jax
import jax.numpy as jnp
from jax import lax
from jax.experimental import pallas as pl
from jax.experimental.pallas import tpu as pltpu
from jax.sharding import PartitionSpec as P

F32 = jnp.float32
BF16 = jnp.bfloat16
MESH = pl.DeviceIdType.MESH
NV = 5


def split(x):
    hi = x.astype(BF16)
    return hi, (x - hi.astype(F32)).astype(BF16)


def tile_group(weights, u, g, count=8):
    hi, lo = split(u)
    left = jnp.concatenate(
        [jnp.concatenate([hi, hi], 1), jnp.concatenate([lo, jnp.zeros_like(lo)], 1)], 0
    )
    out = jnp.dot(left, weights[g, :, 0 : count * 128], preferred_element_type=F32)
    rows = [
        out[k : k + 1, k * 128 : k * 128 + 128] + out[8 + k : 9 + k, k * 128 : k * 128 + 128]
        for k in range(count)
    ]
    return jnp.concatenate(rows, axis=0)


def kernel(
    nf, nm, blocks,
    src_h, ap_h, st_h, ge_h, tiles_h, near_h, bin_h, core_h, bout_h,
    p_h, a_h,
    ext, tiles, ghost, weights, near, bin_v, core, bout,
    vec, img, diag, cnext, cprev, scale, p_v, a_v, far, rows,
    m1, m2, m3, mz,
    lsem, tsem, osem, xsem, bsem, zsem,
):
    me = lax.axis_index("flow")
    owner = lax.axis_index("mech")
    right = lax.rem(me + 1, nf)
    left = lax.rem(me + nf - 1, nf)
    head = me == 0
    tail = me == nf - 1
    groups = blocks // 8
    chunk = blocks // 4
    last = blocks - 1
    own = slice(8, 8 + blocks)
    wide = blocks + 16
    body = slice(8, 8 + wide)
    above = slice(7, 7 + wide)
    below = slice(9, 9 + wide)
    mid = slice(16, 16 + blocks)
    zero_row = jnp.zeros((1, 128), F32)

    loads = []

    def load(i, a, b):
        c = pltpu.make_async_copy(a, b, lsem.at[i])
        c.start()
        loads.append(c)

    for i, ref in enumerate((src_h, ap_h, ge_h, st_h)):
        load(i, ref, ext.at[i, pl.ds(8, blocks)])
    tloads = []
    for q in range(4):
        part = pl.ds(q * chunk, chunk)
        c = pltpu.make_async_copy(tiles_h.at[part], tiles.at[part], tsem.at[q])
        c.start()
        tloads.append(c)
    load(4, bin_h, bin_v)
    load(5, near_h, near)
    load(6, core_h, core)
    load(7, bout_h, bout)

    barrier = pltpu.get_barrier_semaphore()

    def greet(d, carry):
        pl.semaphore_signal(
            barrier, inc=1, device_id={"flow": lax.rem(me + d, nf)}, device_id_type=MESH
        )
        return carry

    lax.fori_loop(1, nf, greet, 0)
    for d in range(1, nm):
        pl.semaphore_signal(
            barrier, inc=1, device_id={"mech": lax.rem(owner + d, nm)}, device_id_type=MESH
        )

    def spread(buf, i, size):
        mine = buf.at[pl.ds(pl.multiple_of(me * size, size), size)] if size > 1 else buf.at[me]

        def one(d, carry):
            pltpu.make_async_remote_copy(
                src_ref=mine,
                dst_ref=mine,
                send_sem=bsem.at[i, 0],
                recv_sem=bsem.at[i, 1],
                device_id={"flow": lax.rem(me + d, nf)},
                device_id_type=MESH,
            ).start()
            return carry

        lax.fori_loop(1, nf, one, 0)

    def gather_wait(buf, i, which, size):
        others = buf.at[pl.ds(0, (nf - 1) * size)]
        pltpu.make_async_copy(others, others, bsem.at[i, which]).wait()

    def slots(buf, row):
        return buf[pl.ds(row, nf, stride=8), :]

    def spot(size):
        return pl.ds(pl.multiple_of(me * size, size), size)

    def dot_row(i, x, y):
        rows[i : i + 1, :] = jnp.sum(x * y, axis=0, keepdims=True)

    def row_sums():
        sums = jnp.sum(rows[...].T, axis=0, keepdims=True)
        return jnp.concatenate([sums, jnp.zeros((1, 96), F32)], axis=1)

    def lane(row, i):
        return jnp.broadcast_to(row[:, i : i + 1], (1, 128))

    def total_of(x):
        x = jnp.sum(x, axis=0, keepdims=True)
        return jnp.broadcast_to(jnp.sum(x, axis=1, keepdims=True), (1, 128))

    rows[...] = jnp.zeros_like(rows)
    m1[pl.ds(nf * 8, 8), :] = jnp.zeros((8, 128), F32)
    m2[pl.ds(nf * 8, 8), :] = jnp.zeros((8, 128), F32)
    for k in range(NV):
        vec[k, 0:8, :] = jnp.zeros((8, 128), F32)
        vec[k, 8 + wide : 16 + wide, :] = jnp.zeros((8, 128), F32)
        img[k, 0:8, :] = jnp.zeros((8, 128), F32)
        img[k, 8 + blocks : wide, :] = jnp.zeros((8, 128), F32)

    for i in range(3):
        loads[i].wait()
    a = ext[1, own, :]
    b = ext[0, own, :]
    s = a * jnp.sqrt(a)
    scale[own, :] = s

    def prepare(tile, g, k):
        hi, lo = split(tile)
        weights[g, 0:128, k * 128 : k * 128 + 128] = hi
        weights[g, 128:256, k * 128 : k * 128 + 128] = lo

    for q in range(4):
        tloads[q].wait()
        for g in range(q * groups // 4, (q + 1) * groups // 4):
            for k in range(8):
                prepare(tiles[g * 8 + k], g, k)
            part = slice(8 + g * 8, 16 + g * 8)
            ext[4, part, :] = tile_group(weights, scale[part, :] * ext[0, part, :], g)

    loads[3].wait()
    cube = a * a * a
    half = ext[2, own, :] * 0.5
    edge = half[last:] * cube[last:]
    inner = half[:last] * (cube[:last] + cube[1:])
    cond = jnp.concatenate([inner, jnp.where(tail, edge, zero_row)], axis=0)
    cp = jnp.concatenate([zero_row, inner], axis=0)
    ahead = jnp.concatenate([b[1:], zero_row], axis=0)
    behind = jnp.concatenate([zero_row, b[:last]], axis=0)
    alone = (ext[3, own, :] + cond + cp) * b + s * ext[4, own, :] - cond * ahead - cp * behind
    dot_row(0, b, b)
    dot_row(1, b, alone)
    dot_row(2, alone, alone)
    m1[spot(8), :] = jnp.concatenate(
        [
            row_sums(),
            jnp.where(tail, zero_row, half[last:]), cube[last:], b[last:], alone[last:],
            cube[0:1], b[0:1], alone[0:1],
        ],
        axis=0,
    )
    pl.semaphore_wait(barrier, nf - 1 + nm - 1)

    pending = []

    def hand_over(a, b, i, dev):
        c = pltpu.make_async_remote_copy(
            src_ref=a, dst_ref=b, send_sem=xsem.at[i, 0], recv_sem=xsem.at[i, 1],
            device_id={"flow": dev}, device_id_type=MESH,
        )
        c.start()
        pending.append(c)

    hand_over(ext.at[:, pl.ds(blocks, 8)], ext.at[:, pl.ds(0, 8)], 0, right)
    hand_over(ext.at[:, pl.ds(8, 8)], ext.at[:, pl.ds(8 + blocks, 8)], 1, left)
    hand_over(tiles.at[pl.ds(blocks - 2, 2)], ghost.at[pl.ds(0, 2)], 2, right)
    hand_over(tiles.at[pl.ds(0, 2)], ghost.at[pl.ds(2, 2)], 3, left)
    spread(m1, 0, 8)
    pending[0].wait_recv()
    pending[1].wait_recv()

    row = lax.broadcasted_iota(jnp.int32, (wide, 128), 0)
    at_tail = row == jnp.where(tail, 7 + blocks, -1)
    at_head = row == jnp.where(head, 7, -1)
    a = ext[1]
    s = a * jnp.sqrt(a)
    scale[...] = s
    cube = a * a * a
    cube_next = jnp.where(at_tail, 0.0, jnp.concatenate([cube[1:], zero_row], axis=0))
    cond = jnp.where(at_head, 0.0, ext[2] * (cube + cube_next) * 0.5)
    cp = jnp.concatenate([zero_row, cond[:-1]], axis=0)
    cnext[...] = jnp.where(at_tail, 0.0, cond)
    cprev[...] = cp
    diag[...] = ext[3] + cond + cp
    vec[0, body, :] = ext[0]
    img[0] = ext[4]

    def finish(k):
        img[k] = (
            diag[...] * vec[k, body, :]
            + scale[...] * img[k]
            - cnext[...] * vec[k, below, :]
            - cprev[...] * vec[k, above, :]
        )

    def product(k):
        for g in range(groups):
            part = slice(8 + g * 8, 16 + g * 8)
            u = scale[part, :] * vec[k, 16 + g * 8 : 24 + g * 8, :]
            img[k, part, :] = tile_group(weights, u, g)

    def ghost_product(k):
        low, high = slice(6, 8), slice(8 + blocks, 10 + blocks)
        u = jnp.concatenate(
            [
                scale[low, :] * vec[k, 14:16, :],
                scale[high, :] * vec[k, 16 + blocks : 18 + blocks, :],
                jnp.zeros((4, 128), F32),
            ],
            axis=0,
        )
        out = tile_group(weights, u, groups, 4)
        img[k, low, :] = out[0:2]
        img[k, high, :] = out[2:4]

    finish(0)
    vec[1, body, :] = img[0]
    product(1)
    pending[2].wait_recv()
    pending[3].wait_recv()
    for k in range(4):
        prepare(ghost[k], groups, k)
    ghost_product(1)
    finish(1)
    gather_wait(m1, 0, 1, 8)

    def following(row):
        return m1[pl.ds(8 + row, nf, stride=8), :]

    total = jnp.sum(slots(m1, 0), axis=0, keepdims=True)
    gap = slots(m1, 3) - following(6)
    flux = slots(m1, 1) * (slots(m1, 2) + following(5)) * gap
    bb = lane(total, 0)
    bw = lane(total, 1) + total_of(flux * gap)
    ww = lane(total, 2) + 2.0 * total_of(flux * (slots(m1, 4) - following(7) + flux))
    mean = bw / bb
    dev = jnp.sqrt(jnp.maximum(ww / bb - mean * mean, (0.01 * mean) * (0.01 * mean)))
    inv = 1.0 / dev
    shifted = (mean + 0.8 * dev) * inv
    w0 = img[0]
    b = ext[0]
    v1 = (w0 - mean * b) * inv
    w1 = (img[1] - mean * w0) * inv
    vec[1, body, :] = v1
    img[1] = w1
    vec[2, body, :] = w1 * inv - shifted * v1 - b
    product(2)
    ghost_product(2)
    finish(2)
    vec[3, body, :] = img[2] * inv - shifted * vec[2, body, :] - vec[1, body, :]
    product(3)
    finish(3)
    vec[4, mid, :] = (
        img[3, own, :] * inv - shifted * vec[3, mid, :] - vec[2, mid, :]
    )
    vec[4, 8:16, :] = jnp.zeros((8, 128), F32)
    vec[4, 16 + blocks : 24 + blocks, :] = jnp.zeros((8, 128), F32)
    product(4)
    finish(4)
    pairs = {}

    def entry(j, k):
        pairs[(j, k)] = len(pairs)
        dot_row(pairs[(j, k)], vec[k, mid, :], img[j, own, :])

    for k in range(NV):
        for j in range(k + 1):
            entry(j, k)
    for k in range(1, NV):
        pairs[("g", k)] = len(pairs)
        dot_row(pairs[("g", k)], vec[k, mid, :], vec[1, mid, :])
    m2[spot(8), :] = jnp.concatenate(
        [
            row_sums(),
            cnext[7 + blocks : 8 + blocks, :] * vec[4, 15 + blocks : 16 + blocks, :],
            vec[4, 16:17, :],
            jnp.zeros((5, 128), F32),
        ],
        axis=0,
    )
    spread(m2, 1, 8)
    loads[4].wait()
    loads[5].wait()
    gather_wait(m2, 1, 1, 8)

    total = jnp.sum(slots(m2, 0), axis=0, keepdims=True)
    cross = total_of(slots(m2, 1) * m2[pl.ds(8 + 2, nf, stride=8), :])
    full = [[None] * NV for _ in range(NV)]
    for j in range(NV):
        for k in range(j, NV):
            full[j][k] = lane(total, pairs[(j, k)])
    full[4][4] = full[4][4] - 2.0 * cross
    size = [full[j][j] for j in range(NV)]
    ratio = -dev / mean
    y = [zero_row] + [ratio * lane(total, pairs[("g", k)]) for k in range(1, NV)]
    low = [[None] * NV for _ in range(NV)]
    pivot = [None] * NV
    for j in range(NV):
        good = full[j][j] > 1e-6 * size[j]
        pivot[j] = jnp.where(good, 1.0 / jnp.where(good, full[j][j], 1.0), 0.0)
        for i in range(j + 1, NV):
            low[i][j] = full[j][i] * pivot[j]
        for i in range(j + 1, NV):
            for k in range(i, NV):
                full[i][k] = full[i][k] - low[i][j] * full[j][k]
            y[i] = y[i] - low[i][j] * y[j]
    coef = [y[j] * pivot[j] for j in range(NV)]
    for j in range(NV - 2, -1, -1):
        for i in range(j + 1, NV):
            coef[j] = coef[j] - low[i][j] * coef[i]
    coef[0] = coef[0] + 1.0 / mean
    p = coef[0] * vec[0, mid, :]
    for k in range(1, NV):
        p = p + coef[k] * vec[k, mid, :]
    p_v[...] = p
    out_p = pltpu.make_async_copy(p_v, p_h, osem.at[0])
    out_p.start()

    acc = jnp.zeros((64, 128), F32)
    for g in range(blocks):
        acc = acc + bin_v[:, g * 128 : g * 128 + 128] * p_v[g : g + 1, :]
    m3[me] = jnp.concatenate(
        [jnp.sum(acc.T, axis=0, keepdims=True), jnp.zeros((1, 64), F32)], axis=1
    )
    spread(m3, 2, 1)

    clusters = blocks // nm
    mine = jnp.zeros((clusters, 128), F32)
    for q in range(nm):
        mine = jnp.where(owner == q, p_v[pl.ds(q, clusters, stride=nm), :], mine)
    mine = mine.astype(BF16)
    per = clusters // 4
    for r in range(4):
        for c in range(r * per, (r + 1) * per):
            full_c = lax.dot_general(
                mine, near[c], (((1,), (1,)), ((), ())), preferred_element_type=F32
            )
            for q in range(nm):
                mz[owner, nm * c + q : nm * c + q + 1, :] = full_c[
                    c : c + 1, q * 128 : q * 128 + 128
                ]
        piece = mz.at[owner, pl.ds(r * per * nm, per * nm)]
        for d in range(1, nm):
            pltpu.make_async_remote_copy(
                src_ref=piece,
                dst_ref=piece,
                send_sem=zsem.at[r, 0],
                recv_sem=zsem.at[r, 1],
                device_id={"mech": lax.rem(owner + d, nm)},
                device_id_type=MESH,
            ).start()

    def z_wait(r, which):
        others = mz.at[pl.ds(0, nm - 1), pl.ds(r * per * nm, per * nm)]
        pltpu.make_async_copy(others, others, zsem.at[r, which]).wait()

    loads[6].wait()
    loads[7].wait()
    gather_wait(m3, 2, 1, 1)
    coeffs = jnp.sum(m3[...], axis=0)[:, 0:64]
    mixed = jnp.sum(core[...] * coeffs, axis=1, keepdims=True)
    mixed = jnp.broadcast_to(mixed, (64, 128))
    for g in range(blocks):
        far[g : g + 1, :] = jnp.sum(
            bout[:, g * 128 : g * 128 + 128] * mixed, axis=0, keepdims=True
        )
    for r in range(4):
        z_wait(r, 1)
    shift = jnp.sum(mz[...], axis=0) + far[...]
    a_v[...] = ext[1, own, :] * (1.0 + 0.5 * jnp.tanh(shift))
    out_a = pltpu.make_async_copy(a_v, a_h, osem.at[1])
    out_a.start()
    for c in pending:
        c.wait_send()
    gather_wait(m1, 0, 0, 8)
    gather_wait(m2, 1, 0, 8)
    gather_wait(m3, 2, 0, 1)
    for r in range(4):
        z_wait(r, 0)
    out_p.wait()
    out_a.wait()


def solution(mesh):
    nf = mesh.shape["flow"]
    nm = mesh.shape["mech"]

    def local(source, aperture_rest, storage, geometry, tiles, near, basis_in, core, basis_out):
        blocks, width = source.shape
        rank = core.shape[0]
        grid = (blocks, width)
        vm = pltpu.VMEM
        wide = (blocks + 16, width)
        scratch = [
            vm((5,) + wide, F32), vm(tiles.shape, F32), vm((4, width, width), F32),
            vm((blocks // 8 + 1, 2 * width, 8 * width), BF16),
            vm(near.shape, BF16), vm((rank, basis_in.shape[0]), F32), vm(core.shape, F32),
            vm((rank, basis_in.shape[0]), F32),
            vm((NV, blocks + 32, width), F32), vm((NV,) + wide, F32),
            vm(wide, F32), vm(wide, F32), vm(wide, F32), vm(wide, F32),
            vm(grid, F32), vm(grid, F32), vm(grid, F32), vm((32, width), F32),
            vm(((nf + 1) * 8, width), F32), vm(((nf + 1) * 8, width), F32),
            vm((nf, 1, width), F32), vm((nm,) + grid, F32),
            pltpu.SemaphoreType.DMA((8,)), pltpu.SemaphoreType.DMA((4,)),
            pltpu.SemaphoreType.DMA((2,)), pltpu.SemaphoreType.DMA((4, 2)),
            pltpu.SemaphoreType.DMA((3, 2)), pltpu.SemaphoreType.DMA((4, 2)),
        ]
        anywhere = pl.BlockSpec(memory_space=pltpu.HBM)
        return pl.pallas_call(
            functools.partial(kernel, nf, nm, blocks),
            out_shape=(jax.ShapeDtypeStruct(grid, F32), jax.ShapeDtypeStruct(grid, F32)),
            in_specs=[anywhere] * 9,
            out_specs=(anywhere, anywhere),
            scratch_shapes=scratch,
            compiler_params=pltpu.CompilerParams(
                collective_id=0, has_side_effects=True, vmem_limit_bytes=63 << 20
            ),
        )(
            source, aperture_rest, storage, geometry, tiles, near,
            basis_in.T, core, basis_out.T,
        )

    placed = (
        P("flow", None), P("flow", None), P("flow", None), P("flow", None),
        P("flow", None, None), P("flow", None, "mech"), P("flow", None), P(), P("flow", None),
    )
    return jax.shard_map(
        local,
        mesh=mesh,
        in_specs=placed,
        out_specs=(P("flow", None), P("flow", None)),
        check_vma=False,
    )
```

```python
import functools
import jax
import jax.numpy as jnp
from jax import lax
from jax.experimental import pallas as pl
from jax.experimental.pallas import tpu as pltpu
from jax.sharding import PartitionSpec as P

F32 = jnp.float32
BF16 = jnp.bfloat16
MESH = pl.DeviceIdType.MESH
NV = 5


def split(x):
    hi = x.astype(BF16)
    return hi, (x - hi.astype(F32)).astype(BF16)


def tile_group(weights, u, g, count=8):
    hi, lo = split(u)
    left = jnp.concatenate(
        [jnp.concatenate([hi, hi], 1), jnp.concatenate([lo, jnp.zeros_like(lo)], 1)], 0
    )
    out = jnp.dot(left, weights[g, :, 0 : count * 128], preferred_element_type=F32)
    rows = [
        out[k : k + 1, k * 128 : k * 128 + 128] + out[8 + k : 9 + k, k * 128 : k * 128 + 128]
        for k in range(count)
    ]
    return jnp.concatenate(rows, axis=0)


def closing(p_in, shift, rest, p_out, a_out):
    p_out[...] = p_in[...]
    a_out[...] = rest[...] * (1.0 + 0.5 * jnp.tanh(shift[...]))


def kernel(
    nf, nm, blocks,
    src_h, ap_h, st_h, ge_h, tiles_h, near_h, bin_h, core_h, bout_h,
    p_h, a_h,
    ext, tiles, ghost, weights, near, bin_v, core, bout,
    vec, img, diag, cnext, cprev, scale, p_v, a_v, far, rows,
    m1, m2, m3, mz,
    lsem, tsem, osem, xsem, bsem, zsem,
):
    me = lax.axis_index("flow")
    owner = lax.axis_index("mech")
    right = lax.rem(me + 1, nf)
    left = lax.rem(me + nf - 1, nf)
    head = me == 0
    tail = me == nf - 1
    groups = blocks // 8
    chunk = blocks // 4
    last = blocks - 1
    own = slice(8, 8 + blocks)
    wide = blocks + 16
    body = slice(8, 8 + wide)
    above = slice(7, 7 + wide)
    below = slice(9, 9 + wide)
    mid = slice(16, 16 + blocks)
    zero_row = jnp.zeros((1, 128), F32)

    loads = []

    def load(i, a, b):
        c = pltpu.make_async_copy(a, b, lsem.at[i])
        c.start()
        loads.append(c)

    for i, ref in enumerate((src_h, ap_h, ge_h, st_h)):
        load(i, ref, ext.at[i, pl.ds(8, blocks)])
    tloads = []
    for q in range(4):
        part = pl.ds(q * chunk, chunk)
        c = pltpu.make_async_copy(tiles_h.at[part], tiles.at[part], tsem.at[q])
        c.start()
        tloads.append(c)
    load(4, bin_h, bin_v)
    load(5, near_h, near)
    load(6, core_h, core)
    load(7, bout_h, bout)

    barrier = pltpu.get_barrier_semaphore()

    def greet(d, carry):
        pl.semaphore_signal(
            barrier, inc=1, device_id={"flow": lax.rem(me + d, nf)}, device_id_type=MESH
        )
        return carry

    lax.fori_loop(1, nf, greet, 0)
    for d in range(1, nm):
        pl.semaphore_signal(
            barrier, inc=1, device_id={"mech": lax.rem(owner + d, nm)}, device_id_type=MESH
        )

    def spread(buf, i, size):
        mine = buf.at[pl.ds(pl.multiple_of(me * size, size), size)] if size > 1 else buf.at[me]

        def one(d, carry):
            pltpu.make_async_remote_copy(
                src_ref=mine,
                dst_ref=mine,
                send_sem=bsem.at[i, 0],
                recv_sem=bsem.at[i, 1],
                device_id={"flow": lax.rem(me + d, nf)},
                device_id_type=MESH,
            ).start()
            return carry

        lax.fori_loop(1, nf, one, 0)

    def gather_wait(buf, i, which, size):
        others = buf.at[pl.ds(0, (nf - 1) * size)]
        pltpu.make_async_copy(others, others, bsem.at[i, which]).wait()

    def slots(buf, row):
        return buf[pl.ds(row, nf, stride=8), :]

    def spot(size):
        return pl.ds(pl.multiple_of(me * size, size), size)

    def dot_row(i, x, y):
        rows[i : i + 1, :] = jnp.sum(x * y, axis=0, keepdims=True)

    def row_sums():
        sums = jnp.sum(rows[...].T, axis=0, keepdims=True)
        return jnp.concatenate([sums, jnp.zeros((1, 96), F32)], axis=1)

    def lane(row, i):
        return jnp.broadcast_to(row[:, i : i + 1], (1, 128))

    def total_of(x):
        x = jnp.sum(x, axis=0, keepdims=True)
        return jnp.broadcast_to(jnp.sum(x, axis=1, keepdims=True), (1, 128))

    rows[...] = jnp.zeros_like(rows)
    m1[pl.ds(nf * 8, 8), :] = jnp.zeros((8, 128), F32)
    m2[pl.ds(nf * 8, 8), :] = jnp.zeros((8, 128), F32)
    for k in range(NV):
        vec[k, 0:8, :] = jnp.zeros((8, 128), F32)
        vec[k, 8 + wide : 16 + wide, :] = jnp.zeros((8, 128), F32)
        img[k, 0:8, :] = jnp.zeros((8, 128), F32)
        img[k, 8 + blocks : wide, :] = jnp.zeros((8, 128), F32)

    for i in range(3):
        loads[i].wait()
    a = ext[1, own, :]
    b = ext[0, own, :]
    s = a * jnp.sqrt(a)
    scale[own, :] = s

    def prepare(tile, g, k):
        hi, lo = split(tile)
        weights[g, 0:128, k * 128 : k * 128 + 128] = hi
        weights[g, 128:256, k * 128 : k * 128 + 128] = lo

    for q in range(4):
        tloads[q].wait()
        for g in range(q * groups // 4, (q + 1) * groups // 4):
            for k in range(8):
                prepare(tiles[g * 8 + k], g, k)
            part = slice(8 + g * 8, 16 + g * 8)
            ext[4, part, :] = tile_group(weights, scale[part, :] * ext[0, part, :], g)

    loads[3].wait()
    cube = a * a * a
    half = ext[2, own, :] * 0.5
    edge = half[last:] * cube[last:]
    inner = half[:last] * (cube[:last] + cube[1:])
    cond = jnp.concatenate([inner, jnp.where(tail, edge, zero_row)], axis=0)
    cp = jnp.concatenate([zero_row, inner], axis=0)
    ahead = jnp.concatenate([b[1:], zero_row], axis=0)
    behind = jnp.concatenate([zero_row, b[:last]], axis=0)
    alone = (ext[3, own, :] + cond + cp) * b + s * ext[4, own, :] - cond * ahead - cp * behind
    dot_row(0, b, b)
    dot_row(1, b, alone)
    dot_row(2, alone, alone)
    m1[spot(8), :] = jnp.concatenate(
        [
            row_sums(),
            jnp.where(tail, zero_row, half[last:]), cube[last:], b[last:], alone[last:],
            cube[0:1], b[0:1], alone[0:1],
        ],
        axis=0,
    )
    pl.semaphore_wait(barrier, nf - 1 + nm - 1)

    pending = []

    def hand_over(a, b, i, dev):
        c = pltpu.make_async_remote_copy(
            src_ref=a, dst_ref=b, send_sem=xsem.at[i, 0], recv_sem=xsem.at[i, 1],
            device_id={"flow": dev}, device_id_type=MESH,
        )
        c.start()
        pending.append(c)

    hand_over(ext.at[:, pl.ds(blocks, 8)], ext.at[:, pl.ds(0, 8)], 0, right)
    hand_over(ext.at[:, pl.ds(8, 8)], ext.at[:, pl.ds(8 + blocks, 8)], 1, left)
    spread(m1, 0, 8)
    hand_over(tiles.at[pl.ds(blocks - 2, 2)], ghost.at[pl.ds(0, 2)], 2, right)
    hand_over(tiles.at[pl.ds(0, 2)], ghost.at[pl.ds(2, 2)], 3, left)
    pending[0].wait_recv()
    pending[1].wait_recv()

    row = lax.broadcasted_iota(jnp.int32, (wide, 128), 0)
    at_tail = row == jnp.where(tail, 7 + blocks, -1)
    at_head = row == jnp.where(head, 7, -1)
    a = ext[1]
    s = a * jnp.sqrt(a)
    scale[...] = s
    cube = a * a * a
    cube_next = jnp.where(at_tail, 0.0, jnp.concatenate([cube[1:], zero_row], axis=0))
    cond = jnp.where(at_head, 0.0, ext[2] * (cube + cube_next) * 0.5)
    cp = jnp.concatenate([zero_row, cond[:-1]], axis=0)
    cnext[...] = jnp.where(at_tail, 0.0, cond)
    cprev[...] = cp
    diag[...] = ext[3] + cond + cp
    vec[0, body, :] = ext[0]
    img[0] = ext[4]

    def finish(k):
        img[k] = (
            diag[...] * vec[k, body, :]
            + scale[...] * img[k]
            - cnext[...] * vec[k, below, :]
            - cprev[...] * vec[k, above, :]
        )

    def product(k):
        for g in range(groups):
            part = slice(8 + g * 8, 16 + g * 8)
            u = scale[part, :] * vec[k, 16 + g * 8 : 24 + g * 8, :]
            img[k, part, :] = tile_group(weights, u, g)

    def ghost_product(k):
        low, high = slice(6, 8), slice(8 + blocks, 10 + blocks)
        u = jnp.concatenate(
            [
                scale[low, :] * vec[k, 14:16, :],
                scale[high, :] * vec[k, 16 + blocks : 18 + blocks, :],
                jnp.zeros((4, 128), F32),
            ],
            axis=0,
        )
        out = tile_group(weights, u, groups, 4)
        img[k, low, :] = out[0:2]
        img[k, high, :] = out[2:4]

    finish(0)
    vec[1, body, :] = img[0]
    product(1)
    pending[2].wait_recv()
    pending[3].wait_recv()
    for k in range(4):
        prepare(ghost[k], groups, k)
    ghost_product(1)
    finish(1)
    gather_wait(m1, 0, 1, 8)

    def following(row):
        return m1[pl.ds(8 + row, nf, stride=8), :]

    total = jnp.sum(slots(m1, 0), axis=0, keepdims=True)
    gap = slots(m1, 3) - following(6)
    flux = slots(m1, 1) * (slots(m1, 2) + following(5)) * gap
    bb = lane(total, 0)
    bw = lane(total, 1) + total_of(flux * gap)
    ww = lane(total, 2) + 2.0 * total_of(flux * (slots(m1, 4) - following(7) + flux))
    mean = bw / bb
    dev = jnp.sqrt(jnp.maximum(ww / bb - mean * mean, (0.01 * mean) * (0.01 * mean)))
    inv = 1.0 / dev
    shifted = (mean + 0.8 * dev) * inv
    w0 = img[0]
    b = ext[0]
    v1 = (w0 - mean * b) * inv
    w1 = (img[1] - mean * w0) * inv
    vec[1, body, :] = v1
    img[1] = w1
    vec[2, body, :] = w1 * inv - shifted * v1 - b
    product(2)
    ghost_product(2)
    finish(2)
    vec[3, body, :] = img[2] * inv - shifted * vec[2, body, :] - vec[1, body, :]
    product(3)
    finish(3)
    vec[4, mid, :] = (
        img[3, own, :] * inv - shifted * vec[3, mid, :] - vec[2, mid, :]
    )
    vec[4, 8:16, :] = jnp.zeros((8, 128), F32)
    vec[4, 16 + blocks : 24 + blocks, :] = jnp.zeros((8, 128), F32)
    product(4)
    finish(4)
    pairs = {}

    def entry(j, k):
        pairs[(j, k)] = len(pairs)
        dot_row(pairs[(j, k)], vec[k, mid, :], img[j, own, :])

    for k in range(NV):
        for j in range(k + 1):
            entry(j, k)
    for k in range(1, NV):
        pairs[("g", k)] = len(pairs)
        dot_row(pairs[("g", k)], vec[k, mid, :], vec[1, mid, :])
    m2[spot(8), :] = jnp.concatenate(
        [
            row_sums(),
            cnext[7 + blocks : 8 + blocks, :] * vec[4, 15 + blocks : 16 + blocks, :],
            vec[4, 16:17, :],
            jnp.zeros((5, 128), F32),
        ],
        axis=0,
    )
    spread(m2, 1, 8)
    loads[4].wait()
    loads[5].wait()
    accs = [jnp.zeros((64, 128), F32)] * NV
    for g in range(blocks):
        cut = bin_v[:, g * 128 : g * 128 + 128]
        accs = [accs[k] + cut * vec[k, 16 + g : 17 + g, :] for k in range(NV)]
    far_rows = [jnp.sum(acc.T, axis=0, keepdims=True) for acc in accs] + [zero_row[:, 0:64]]
    m3[spot(8), :] = jnp.concatenate(
        [jnp.concatenate(far_rows[i : i + 2], axis=1) for i in (0, 2, 4)]
        + [jnp.zeros((5, 128), F32)],
        axis=0,
    )
    spread(m3, 2, 8)
    gather_wait(m2, 1, 1, 8)

    total = jnp.sum(slots(m2, 0), axis=0, keepdims=True)
    cross = total_of(slots(m2, 1) * m2[pl.ds(8 + 2, nf, stride=8), :])
    full = [[None] * NV for _ in range(NV)]
    for j in range(NV):
        for k in range(j, NV):
            full[j][k] = lane(total, pairs[(j, k)])
    full[4][4] = full[4][4] - 2.0 * cross
    size = [full[j][j] for j in range(NV)]
    ratio = -dev / mean
    y = [zero_row] + [ratio * lane(total, pairs[("g", k)]) for k in range(1, NV)]
    low = [[None] * NV for _ in range(NV)]
    pivot = [None] * NV
    for j in range(NV):
        good = full[j][j] > 1e-6 * size[j]
        pivot[j] = jnp.where(good, 1.0 / jnp.where(good, full[j][j], 1.0), 0.0)
        for i in range(j + 1, NV):
            low[i][j] = full[j][i] * pivot[j]
        for i in range(j + 1, NV):
            for k in range(i, NV):
                full[i][k] = full[i][k] - low[i][j] * full[j][k]
            y[i] = y[i] - low[i][j] * y[j]
    coef = [y[j] * pivot[j] for j in range(NV)]
    for j in range(NV - 2, -1, -1):
        for i in range(j + 1, NV):
            coef[j] = coef[j] - low[i][j] * coef[i]
    coef[0] = coef[0] + 1.0 / mean
    p = coef[0] * vec[0, mid, :]
    for k in range(1, NV):
        p = p + coef[k] * vec[k, mid, :]
    p_v[...] = p
    out_p = pltpu.make_async_copy(p_v, p_h, osem.at[0])
    out_p.start()

    clusters = blocks // nm
    mine = jnp.zeros((clusters, 128), F32)
    for q in range(nm):
        mine = jnp.where(owner == q, p_v[pl.ds(q, clusters, stride=nm), :], mine)
    mine = mine.astype(BF16)
    per = clusters // 4
    for r in range(4):
        for c in range(r * per, (r + 1) * per):
            full_c = lax.dot_general(
                mine, near[c], (((1,), (1,)), ((), ())), preferred_element_type=F32
            )
            for q in range(nm):
                mz[owner, nm * c + q : nm * c + q + 1, :] = full_c[
                    c : c + 1, q * 128 : q * 128 + 128
                ]
        piece = mz.at[owner, pl.ds(r * per * nm, per * nm)]
        for d in range(1, nm):
            pltpu.make_async_remote_copy(
                src_ref=piece,
                dst_ref=piece,
                send_sem=zsem.at[r, 0],
                recv_sem=zsem.at[r, 1],
                device_id={"mech": lax.rem(owner + d, nm)},
                device_id_type=MESH,
            ).start()
    def z_wait(r, which):
        others = mz.at[pl.ds(0, nm - 1), pl.ds(r * per * nm, per * nm)]
        pltpu.make_async_copy(others, others, zsem.at[r, which]).wait()

    loads[6].wait()
    loads[7].wait()
    gather_wait(m3, 2, 1, 8)
    lower = lax.broadcasted_iota(jnp.int32, (1, 128), 1) < 64
    parts = [jnp.sum(slots(m3, i), axis=0, keepdims=True) for i in range(3)]
    both = (
        jnp.where(lower, coef[0], coef[1]) * parts[0]
        + jnp.where(lower, coef[2], coef[3]) * parts[1]
        + coef[4] * parts[2]
    )
    coeffs = both[:, 0:64] + both[:, 64:128]
    mixed = jnp.sum(core[...] * coeffs, axis=1, keepdims=True)
    mixed = jnp.broadcast_to(mixed, (64, 128))
    for g in range(blocks):
        far[g : g + 1, :] = jnp.sum(
            bout[:, g * 128 : g * 128 + 128] * mixed, axis=0, keepdims=True
        )
    for r in range(4):
        z_wait(r, 1)
    a_v[...] = jnp.sum(mz[...], axis=0) + far[...]
    out_a = pltpu.make_async_copy(a_v, a_h, osem.at[1])
    out_a.start()
    for c in pending:
        c.wait_send()
    gather_wait(m1, 0, 0, 8)
    gather_wait(m2, 1, 0, 8)
    gather_wait(m3, 2, 0, 8)
    for r in range(4):
        z_wait(r, 0)
    out_p.wait()
    out_a.wait()


def solution(mesh):
    nf = mesh.shape["flow"]
    nm = mesh.shape["mech"]

    def local(source, aperture_rest, storage, geometry, tiles, near, basis_in, core, basis_out):
        blocks, width = source.shape
        rank = core.shape[0]
        grid = (blocks, width)
        vm = pltpu.VMEM
        wide = (blocks + 16, width)
        scratch = [
            vm((5,) + wide, F32), vm(tiles.shape, F32), vm((4, width, width), F32),
            vm((blocks // 8 + 1, 2 * width, 8 * width), BF16),
            vm(near.shape, BF16), vm((rank, basis_in.shape[0]), F32), vm(core.shape, F32),
            vm((rank, basis_in.shape[0]), F32),
            vm((NV, blocks + 32, width), F32), vm((NV,) + wide, F32),
            vm(wide, F32), vm(wide, F32), vm(wide, F32), vm(wide, F32),
            vm(grid, F32), vm(grid, F32), vm(grid, F32), vm((32, width), F32),
            vm(((nf + 1) * 8, width), F32), vm(((nf + 1) * 8, width), F32),
            vm((nf * 8, width), F32), vm((nm,) + grid, F32),
            pltpu.SemaphoreType.DMA((8,)), pltpu.SemaphoreType.DMA((4,)),
            pltpu.SemaphoreType.DMA((2,)), pltpu.SemaphoreType.DMA((4, 2)),
            pltpu.SemaphoreType.DMA((3, 2)), pltpu.SemaphoreType.DMA((4, 2)),
        ]
        anywhere = pl.BlockSpec(memory_space=pltpu.HBM)
        pressure, shift = pl.pallas_call(
            functools.partial(kernel, nf, nm, blocks),
            out_shape=(jax.ShapeDtypeStruct(grid, F32), jax.ShapeDtypeStruct(grid, F32)),
            in_specs=[anywhere] * 9,
            out_specs=(anywhere, anywhere),
            scratch_shapes=scratch,
            compiler_params=pltpu.CompilerParams(
                collective_id=0, has_side_effects=True, vmem_limit_bytes=63 << 20
            ),
        )(
            source, aperture_rest, storage, geometry, tiles, near,
            basis_in.T, core, basis_out.T,
        )
        return pl.pallas_call(
            closing,
            out_shape=(jax.ShapeDtypeStruct(grid, F32), jax.ShapeDtypeStruct(grid, F32)),
            in_specs=[pl.BlockSpec(memory_space=pltpu.VMEM)] * 3,
            out_specs=(pl.BlockSpec(memory_space=pltpu.VMEM),) * 2,
        )(pressure, shift, aperture_rest)

    placed = (
        P("flow", None), P("flow", None), P("flow", None), P("flow", None),
        P("flow", None, None), P("flow", None, "mech"), P("flow", None), P(), P("flow", None),
    )
    return jax.shard_map(
        local,
        mesh=mesh,
        in_specs=placed,
        out_specs=(P("flow", None), P("flow", None)),
        check_vma=False,
    )
```

```python
import functools
import jax
import jax.numpy as jnp
from jax import lax
from jax.experimental import pallas as pl
from jax.experimental.pallas import tpu as pltpu
from jax.sharding import PartitionSpec as P

F32 = jnp.float32
BF16 = jnp.bfloat16
MESH = pl.DeviceIdType.MESH
NV = 5
LEAST = 5e-5


def split(x):
    hi = x.astype(BF16)
    return hi, (x - hi.astype(F32)).astype(BF16)


CG = 5


def extended(cells, sides, width):
    for axis, dim in sides:
        count = lax.axis_size(axis)
        ends = count - 1
        head = lax.slice_in_dim(cells, 0, width, axis=dim)
        tail = lax.slice_in_dim(cells, cells.shape[dim] - width, cells.shape[dim], axis=dim)
        cells = jnp.concatenate(
            [
                lax.ppermute(tail, axis, [(i, (i + 1) % count) for i in range(ends)]),
                cells,
                lax.ppermute(head, axis, [((i + 1) % count, i) for i in range(ends)]),
            ],
            axis=dim,
        )
    return cells


def exchange_faces(v):
    return extended(v, (("flow", 0),), 1)


def operate(v, tiles, scale, storage, cond_all):
    padded = exchange_faces(v)
    local = jnp.einsum("bij,bj->bi", tiles, scale * v, precision=lax.Precision.HIGHEST) * scale
    cond = cond_all[1:]
    cprv = cond_all[:-1]
    return storage * v + local + (cond + cprv) * v - cond * padded[2:] - cprv * padded[:-2]


def squares(residual):
    return lax.psum(jnp.sum(residual * residual), "flow")


def curving(direction, image):
    return lax.psum(jnp.sum(direction * image), "flow")


def solve_flow(source, tiles, scale, storage, cond_all):
    pressure = jnp.zeros_like(source)
    residual = source
    direction = source
    norm_now = squares(residual)
    for step in range(CG):
        image = operate(direction, tiles, scale, storage, cond_all)
        alpha = norm_now / curving(direction, image)
        pressure = pressure + alpha * direction
        residual = residual - alpha * image
        norm_next = squares(residual)
        direction = residual + norm_next / norm_now * direction
        norm_now = norm_next
    return pressure


def plain(source, aperture_rest, storage, geometry, tiles, near, basis_in, core, basis_out):
    blocks, width = source.shape
    groups = lax.axis_size("mech")
    owner = lax.axis_index("mech")
    clusters = near.shape[0]
    span = near.shape[2]
    aperture = aperture_rest
    stacked = jnp.stack([aperture, geometry])
    padded = extended(stacked, (("flow", 1),), 1)
    ap_pad = padded[0]
    geo_pad = padded[1]
    cond_all = geo_pad[:-1] * (ap_pad[:-1] ** 3 + ap_pad[1:] ** 3) * 0.5
    scale = aperture**1.5
    pressure = solve_flow(source, tiles, scale, storage, cond_all)
    packed = pressure.astype(jnp.bfloat16).reshape(clusters, span * groups)
    piece = lax.dynamic_slice_in_dim(packed, owner * span, span, 1)
    partial_value = jnp.einsum(
        "cij,cj->ci", near, piece, preferred_element_type=jnp.float32
    ).reshape(blocks, width)
    coeffs = lax.psum(
        jnp.dot(pressure.reshape(-1), basis_in, precision=lax.Precision.HIGHEST), "flow"
    )
    mixed = jnp.dot(core, coeffs, precision=lax.Precision.HIGHEST)
    near_disp = lax.psum(partial_value, "mech")
    far_disp = jnp.dot(basis_out, mixed, precision=lax.Precision.HIGHEST).reshape(blocks, width)
    aperture = aperture_rest * (1.0 + 0.5 * jnp.tanh(near_disp + far_disp))
    return (pressure, aperture)


def tile_group(weights, u, g, count=8):
    hi, lo = split(u)
    left = jnp.concatenate(
        [jnp.concatenate([hi, hi], 1), jnp.concatenate([lo, jnp.zeros_like(lo)], 1)], 0
    )
    out = jnp.dot(left, weights[g, :, 0 : count * 128], preferred_element_type=F32)
    rows = [
        out[k : k + 1, k * 128 : k * 128 + 128] + out[8 + k : 9 + k, k * 128 : k * 128 + 128]
        for k in range(count)
    ]
    return jnp.concatenate(rows, axis=0)


def closing(p_in, shift, rest, p_out, a_out):
    p_out[...] = p_in[...]
    a_out[...] = rest[...] * (1.0 + 0.5 * jnp.tanh(shift[...]))


def kernel(
    nf, nm, blocks,
    src_h, ap_h, st_h, ge_h, tiles_h, near_h, bin_h, core_h, bout_h,
    p_h, a_h, f_h,
    ext, tiles, ghost, weights, near, bin_v, core, bout,
    vec, img, diag, cnext, cprev, scale, p_v, a_v, f_v, far, rows,
    m1, m2, m3, mz,
    lsem, tsem, osem, xsem, bsem, zsem,
):
    me = lax.axis_index("flow")
    owner = lax.axis_index("mech")
    right = lax.rem(me + 1, nf)
    left = lax.rem(me + nf - 1, nf)
    head = me == 0
    tail = me == nf - 1
    groups = blocks // 8
    chunk = blocks // 4
    last = blocks - 1
    own = slice(8, 8 + blocks)
    wide = blocks + 16
    body = slice(8, 8 + wide)
    above = slice(7, 7 + wide)
    below = slice(9, 9 + wide)
    mid = slice(16, 16 + blocks)
    zero_row = jnp.zeros((1, 128), F32)

    loads = []

    def load(i, a, b):
        c = pltpu.make_async_copy(a, b, lsem.at[i])
        c.start()
        loads.append(c)

    for i, ref in enumerate((src_h, ap_h, ge_h, st_h)):
        load(i, ref, ext.at[i, pl.ds(8, blocks)])
    tloads = []
    for q in range(4):
        part = pl.ds(q * chunk, chunk)
        c = pltpu.make_async_copy(tiles_h.at[part], tiles.at[part], tsem.at[q])
        c.start()
        tloads.append(c)

    barrier = pltpu.get_barrier_semaphore()

    def greet(d, carry):
        pl.semaphore_signal(
            barrier, inc=1, device_id={"flow": lax.rem(me + d, nf)}, device_id_type=MESH
        )
        return carry

    lax.fori_loop(1, nf, greet, 0)
    for d in range(1, nm):
        pl.semaphore_signal(
            barrier, inc=1, device_id={"mech": lax.rem(owner + d, nm)}, device_id_type=MESH
        )

    def spread(buf, i, size):
        mine = buf.at[pl.ds(pl.multiple_of(me * 8, 8), size)]

        def one(d, carry):
            pltpu.make_async_remote_copy(
                src_ref=mine,
                dst_ref=mine,
                send_sem=bsem.at[i, 0],
                recv_sem=bsem.at[i, 1],
                device_id={"flow": lax.rem(me + d, nf)},
                device_id_type=MESH,
            ).start()
            return carry

        lax.fori_loop(1, nf, one, 0)

    def gather_wait(buf, i, which, size):
        others = buf.at[pl.ds(0, (nf - 1) * size)]
        pltpu.make_async_copy(others, others, bsem.at[i, which]).wait()

    def slots(buf, row):
        return buf[pl.ds(row, nf, stride=8), :]

    def spot():
        return pl.ds(pl.multiple_of(me * 8, 8), 8)

    def dot_row(i, x, y):
        rows[i : i + 1, :] = jnp.sum(x * y, axis=0, keepdims=True)

    def row_sums():
        sums = jnp.sum(rows[...].T, axis=0, keepdims=True)
        return jnp.concatenate([sums, jnp.zeros((1, 96), F32)], axis=1)

    def lane(row, i):
        return jnp.broadcast_to(row[:, i : i + 1], (1, 128))

    def total_of(x):
        x = jnp.sum(x, axis=0, keepdims=True)
        return jnp.broadcast_to(jnp.sum(x, axis=1, keepdims=True), (1, 128))

    rows[...] = jnp.zeros_like(rows)
    m1[pl.ds(nf * 8, 8), :] = jnp.zeros((8, 128), F32)
    m2[pl.ds(nf * 8, 8), :] = jnp.zeros((8, 128), F32)
    for k in range(NV):
        vec[k, 0:8, :] = jnp.zeros((8, 128), F32)
        vec[k, 8 + wide : 16 + wide, :] = jnp.zeros((8, 128), F32)
        img[k, 0:8, :] = jnp.zeros((8, 128), F32)
        img[k, 8 + blocks : wide, :] = jnp.zeros((8, 128), F32)

    for i in range(3):
        loads[i].wait()
    a = ext[1, own, :]
    b = ext[0, own, :]
    s = a * jnp.sqrt(a)
    scale[own, :] = s

    def prepare(tile, g, k):
        hi, lo = split(tile)
        weights[g, 0:128, k * 128 : k * 128 + 128] = hi
        weights[g, 128:256, k * 128 : k * 128 + 128] = lo

    for q in range(4):
        tloads[q].wait()
        for g in range(q * groups // 4, (q + 1) * groups // 4):
            for k in range(8):
                prepare(tiles[g * 8 + k], g, k)
            part = slice(8 + g * 8, 16 + g * 8)
            ext[4, part, :] = tile_group(weights, scale[part, :] * ext[0, part, :], g)

    load(4, bin_h, bin_v)
    load(5, near_h, near)
    load(6, core_h, core)
    load(7, bout_h, bout)
    loads[3].wait()
    cube = a * a * a
    half = ext[2, own, :] * 0.5
    edge = half[last:] * cube[last:]
    inner = half[:last] * (cube[:last] + cube[1:])
    cond = jnp.concatenate([inner, jnp.where(tail, edge, zero_row)], axis=0)
    cp = jnp.concatenate([zero_row, inner], axis=0)
    ahead = jnp.concatenate([b[1:], zero_row], axis=0)
    behind = jnp.concatenate([zero_row, b[:last]], axis=0)
    alone = (ext[3, own, :] + cond + cp) * b + s * ext[4, own, :] - cond * ahead - cp * behind
    dot_row(0, b, b)
    dot_row(1, b, alone)
    dot_row(2, alone, alone)
    rows[3:4, :] = jnp.where(tail, zero_row, half[last:]) * (1.0 / 128.0)
    rows[4:5, :] = cube[last:] * (1.0 / 128.0)
    rows[5:6, :] = cube[0:1] * (1.0 / 128.0)
    m1[spot(), :] = jnp.concatenate(
        [row_sums(), b[last:], b[0:1], jnp.zeros((5, 128), F32)], axis=0
    )
    pl.semaphore_wait(barrier, nf - 1 + nm - 1)

    pending = []

    def hand_over(a, b, i, dev):
        c = pltpu.make_async_remote_copy(
            src_ref=a, dst_ref=b, send_sem=xsem.at[i, 0], recv_sem=xsem.at[i, 1],
            device_id={"flow": dev}, device_id_type=MESH,
        )
        c.start()
        pending.append(c)

    hand_over(ext.at[:, pl.ds(blocks, 8)], ext.at[:, pl.ds(0, 8)], 0, right)
    hand_over(ext.at[:, pl.ds(8, 8)], ext.at[:, pl.ds(8 + blocks, 8)], 1, left)
    spread(m1, 0, 3)
    hand_over(tiles.at[pl.ds(blocks - 2, 2)], ghost.at[pl.ds(0, 2)], 2, right)
    hand_over(tiles.at[pl.ds(0, 2)], ghost.at[pl.ds(2, 2)], 3, left)
    pending[0].wait_recv()
    pending[1].wait_recv()

    row = lax.broadcasted_iota(jnp.int32, (wide, 128), 0)
    at_tail = row == jnp.where(tail, 7 + blocks, -1)
    at_head = row == jnp.where(head, 7, -1)
    a = ext[1]
    s = a * jnp.sqrt(a)
    scale[...] = s
    cube = a * a * a
    cube_next = jnp.where(at_tail, 0.0, jnp.concatenate([cube[1:], zero_row], axis=0))
    cond = jnp.where(at_head, 0.0, ext[2] * (cube + cube_next) * 0.5)
    cp = jnp.concatenate([zero_row, cond[:-1]], axis=0)
    cnext[...] = jnp.where(at_tail, 0.0, cond)
    cprev[...] = cp
    diag[...] = ext[3] + cond + cp
    vec[0, body, :] = ext[0]
    img[0] = ext[4]

    def finish(k):
        img[k] = (
            diag[...] * vec[k, body, :]
            + scale[...] * img[k]
            - cnext[...] * vec[k, below, :]
            - cprev[...] * vec[k, above, :]
        )

    def product(k):
        for g in range(groups):
            part = slice(8 + g * 8, 16 + g * 8)
            u = scale[part, :] * vec[k, 16 + g * 8 : 24 + g * 8, :]
            img[k, part, :] = tile_group(weights, u, g)

    def ghost_product(k):
        low, high = slice(6, 8), slice(8 + blocks, 10 + blocks)
        u = jnp.concatenate(
            [
                scale[low, :] * vec[k, 14:16, :],
                scale[high, :] * vec[k, 16 + blocks : 18 + blocks, :],
                jnp.zeros((4, 128), F32),
            ],
            axis=0,
        )
        out = tile_group(weights, u, groups, 4)
        img[k, low, :] = out[0:2]
        img[k, high, :] = out[2:4]

    finish(0)
    vec[1, body, :] = img[0]
    product(1)
    pending[2].wait_recv()
    pending[3].wait_recv()
    for k in range(4):
        prepare(ghost[k], groups, k)
    ghost_product(1)
    finish(1)
    gather_wait(m1, 0, 1, 3)

    def following(row):
        return m1[pl.ds(8 + row, nf, stride=8), :]

    sums = slots(m1, 0)
    total = jnp.sum(sums, axis=0, keepdims=True)
    gap = slots(m1, 1) - following(2)
    flux = sums[:, 3:4] * (sums[:, 4:5] + following(0)[:, 5:6]) * gap
    bb = lane(total, 0)
    bw = lane(total, 1) + total_of(flux * gap)
    ww = lane(total, 2) + 2.0 * total_of(flux * (lane(total, 1) / bb * gap + flux))
    mean = bw / bb
    dev = jnp.sqrt(jnp.maximum(ww / bb - mean * mean, (0.01 * mean) * (0.01 * mean)))
    inv = 1.0 / dev
    shifted = (mean + 0.8 * dev) * inv
    w0 = img[0]
    b = ext[0]
    v1 = (w0 - mean * b) * inv
    w1 = (img[1] - mean * w0) * inv
    vec[1, body, :] = v1
    img[1] = w1
    vec[2, body, :] = w1 * inv - shifted * v1 - b
    product(2)
    ghost_product(2)
    finish(2)
    vec[3, body, :] = img[2] * inv - shifted * vec[2, body, :] - vec[1, body, :]
    product(3)
    finish(3)
    vec[4, mid, :] = (
        img[3, own, :] * inv - shifted * vec[3, mid, :] - vec[2, mid, :]
    )
    vec[4, 8:16, :] = jnp.zeros((8, 128), F32)
    vec[4, 16 + blocks : 24 + blocks, :] = jnp.zeros((8, 128), F32)
    product(4)
    finish(4)
    pairs = {}

    def entry(j, k):
        pairs[(j, k)] = len(pairs)
        dot_row(pairs[(j, k)], vec[k, mid, :], img[j, own, :])

    for k in range(NV):
        for j in range(k + 1):
            entry(j, k)
    for k in range(NV):
        pairs[("g", k)] = len(pairs)
        dot_row(pairs[("g", k)], vec[k, mid, :], vec[1, mid, :])
    m2[spot(), :] = jnp.concatenate(
        [
            row_sums(),
            cnext[7 + blocks : 8 + blocks, :] * vec[4, 15 + blocks : 16 + blocks, :],
            vec[4, 16:17, :],
            jnp.zeros((5, 128), F32),
        ],
        axis=0,
    )
    spread(m2, 1, 3)
    loads[4].wait()
    loads[5].wait()
    accs = [jnp.zeros((64, 128), F32)] * NV
    for g in range(blocks):
        cut = bin_v[:, g * 128 : g * 128 + 128]
        accs = [accs[k] + cut * vec[k, 16 + g : 17 + g, :] for k in range(NV)]
    far_rows = [jnp.sum(acc.T, axis=0, keepdims=True) for acc in accs] + [zero_row[:, 0:64]]
    m3[spot(), :] = jnp.concatenate(
        [jnp.concatenate(far_rows[i : i + 2], axis=1) for i in (0, 2, 4)]
        + [jnp.zeros((5, 128), F32)],
        axis=0,
    )
    spread(m3, 2, 3)
    gather_wait(m2, 1, 1, 3)

    total = jnp.sum(slots(m2, 0), axis=0, keepdims=True)
    cross = total_of(slots(m2, 1) * m2[pl.ds(8 + 2, nf, stride=8), :])
    full = [[None] * NV for _ in range(NV)]
    for j in range(NV):
        for k in range(j, NV):
            full[j][k] = lane(total, pairs[(j, k)])
    full[4][4] = full[4][4] - 2.0 * cross
    size = [full[j][j] for j in range(NV)]
    ratio = -dev / mean
    y = [ratio * lane(total, pairs[("g", k)]) for k in range(NV)]
    low = [[None] * NV for _ in range(NV)]
    pivot = [None] * NV
    least = None
    for j in range(NV):
        pivot[j] = 1.0 / full[j][j]
        margin = full[j][j] - LEAST * size[j]
        least = margin if j == 0 else jnp.minimum(least, margin)
        for i in range(j + 1, NV):
            low[i][j] = full[j][i] * pivot[j]
        for i in range(j + 1, NV):
            for k in range(i, NV):
                full[i][k] = full[i][k] - low[i][j] * full[j][k]
            y[i] = y[i] - low[i][j] * y[j]
    coef = [y[j] * pivot[j] for j in range(NV)]
    for j in range(NV - 2, -1, -1):
        for i in range(j + 1, NV):
            coef[j] = coef[j] - low[i][j] * coef[i]
    coef[0] = coef[0] + 1.0 / mean
    p = coef[0] * vec[0, mid, :]
    for k in range(1, NV):
        p = p + coef[k] * vec[k, mid, :]
    p_v[...] = p
    f_h[0, 0] = least[0, 0]
    out_p = pltpu.make_async_copy(p_v, p_h, osem.at[0])
    out_p.start()

    clusters = blocks // nm
    mine = jnp.zeros((clusters, 128), F32)
    for q in range(nm):
        mine = jnp.where(owner == q, p_v[pl.ds(q, clusters, stride=nm), :], mine)
    mine = mine.astype(BF16)
    per = clusters // 4
    for r in range(4):
        for c in range(r * per, (r + 1) * per):
            full_c = lax.dot_general(
                mine, near[c], (((1,), (1,)), ((), ())), preferred_element_type=F32
            )
            for q in range(nm):
                mz[owner, nm * c + q : nm * c + q + 1, :] = full_c[
                    c : c + 1, q * 128 : q * 128 + 128
                ]
        piece = mz.at[owner, pl.ds(r * per * nm, per * nm)]
        for d in range(1, nm):
            pltpu.make_async_remote_copy(
                src_ref=piece,
                dst_ref=piece,
                send_sem=zsem.at[r, 0],
                recv_sem=zsem.at[r, 1],
                device_id={"mech": lax.rem(owner + d, nm)},
                device_id_type=MESH,
            ).start()
    def z_wait(r, which):
        others = mz.at[pl.ds(0, nm - 1), pl.ds(r * per * nm, per * nm)]
        pltpu.make_async_copy(others, others, zsem.at[r, which]).wait()

    loads[6].wait()
    loads[7].wait()
    gather_wait(m3, 2, 1, 3)
    lower = lax.broadcasted_iota(jnp.int32, (1, 128), 1) < 64
    parts = [jnp.sum(slots(m3, i), axis=0, keepdims=True) for i in range(3)]
    both = (
        jnp.where(lower, coef[0], coef[1]) * parts[0]
        + jnp.where(lower, coef[2], coef[3]) * parts[1]
        + coef[4] * parts[2]
    )
    coeffs = both[:, 0:64] + both[:, 64:128]
    mixed = jnp.sum(core[...] * coeffs, axis=1, keepdims=True)
    mixed = jnp.broadcast_to(mixed, (64, 128))
    for g in range(blocks):
        far[g : g + 1, :] = jnp.sum(
            bout[:, g * 128 : g * 128 + 128] * mixed, axis=0, keepdims=True
        )
    for r in range(4):
        z_wait(r, 1)
    a_v[...] = jnp.sum(mz[...], axis=0) + far[...]
    out_a = pltpu.make_async_copy(a_v, a_h, osem.at[1])
    out_a.start()
    for c in pending:
        c.wait_send()
    gather_wait(m1, 0, 0, 3)
    gather_wait(m2, 1, 0, 3)
    gather_wait(m3, 2, 0, 3)
    for r in range(4):
        z_wait(r, 0)
    out_p.wait()
    out_a.wait()


def solution(mesh):
    nf = mesh.shape["flow"]
    nm = mesh.shape["mech"]

    def local(source, aperture_rest, storage, geometry, tiles, near, basis_in, core, basis_out):
        blocks, width = source.shape
        rank = core.shape[0]
        grid = (blocks, width)
        vm = pltpu.VMEM
        wide = (blocks + 16, width)
        scratch = [
            vm((5,) + wide, F32), vm(tiles.shape, F32), vm((4, width, width), F32),
            vm((blocks // 8 + 1, 2 * width, 8 * width), BF16),
            vm(near.shape, BF16), vm((rank, basis_in.shape[0]), F32), vm(core.shape, F32),
            vm((rank, basis_in.shape[0]), F32),
            vm((NV, blocks + 32, width), F32), vm((NV,) + wide, F32),
            vm(wide, F32), vm(wide, F32), vm(wide, F32), vm(wide, F32),
            vm(grid, F32), vm(grid, F32), vm((8, width), F32), vm(grid, F32), vm((32, width), F32),
            vm(((nf + 1) * 8, width), F32), vm(((nf + 1) * 8, width), F32),
            vm((nf * 8, width), F32), vm((nm,) + grid, F32),
            pltpu.SemaphoreType.DMA((8,)), pltpu.SemaphoreType.DMA((4,)),
            pltpu.SemaphoreType.DMA((3,)), pltpu.SemaphoreType.DMA((4, 2)),
            pltpu.SemaphoreType.DMA((3, 2)), pltpu.SemaphoreType.DMA((4, 2)),
        ]
        anywhere = pl.BlockSpec(memory_space=pltpu.HBM)
        pressure, shift, margin = pl.pallas_call(
            functools.partial(kernel, nf, nm, blocks),
            out_shape=(
                jax.ShapeDtypeStruct(grid, F32),
                jax.ShapeDtypeStruct(grid, F32),
                jax.ShapeDtypeStruct((1, 1), F32),
            ),
            in_specs=[anywhere] * 9,
            out_specs=(anywhere, anywhere, pl.BlockSpec(memory_space=pltpu.SMEM)),
            scratch_shapes=scratch,
            compiler_params=pltpu.CompilerParams(
                collective_id=0, has_side_effects=True, vmem_limit_bytes=63 << 20
            ),
        )(
            source, aperture_rest, storage, geometry, tiles, near,
            basis_in.T, core, basis_out.T,
        )
        end = pl.pallas_call(
            closing,
            out_shape=(jax.ShapeDtypeStruct(grid, F32), jax.ShapeDtypeStruct(grid, F32)),
            in_specs=[pl.BlockSpec(memory_space=pltpu.VMEM)] * 3,
            out_specs=(pl.BlockSpec(memory_space=pltpu.VMEM),) * 2,
        )
        return lax.cond(
            margin[0, 0] > 0.0,
            lambda: end(pressure, shift, aperture_rest),
            lambda: plain(
                source, aperture_rest, storage, geometry, tiles, near, basis_in, core, basis_out
            ),
        )

    placed = (
        P("flow", None), P("flow", None), P("flow", None), P("flow", None),
        P("flow", None, None), P("flow", None, "mech"), P("flow", None), P(), P("flow", None),
    )
    return jax.shard_map(
        local,
        mesh=mesh,
        in_specs=placed,
        out_specs=(P("flow", None), P("flow", None)),
        check_vma=False,
    )
```

```python
import functools
import jax
import jax.numpy as jnp
from jax import lax
from jax.experimental import pallas as pl
from jax.experimental.pallas import tpu as pltpu
from jax.sharding import PartitionSpec as P

F32 = jnp.float32
BF16 = jnp.bfloat16
MESH = pl.DeviceIdType.MESH
NV = 5
LEAST = 5e-5


def split(x):
    hi = x.astype(BF16)
    return hi, (x - hi.astype(F32)).astype(BF16)


CG = 5


def extended(cells, sides, width):
    for axis, dim in sides:
        count = lax.axis_size(axis)
        ends = count - 1
        head = lax.slice_in_dim(cells, 0, width, axis=dim)
        tail = lax.slice_in_dim(cells, cells.shape[dim] - width, cells.shape[dim], axis=dim)
        cells = jnp.concatenate(
            [
                lax.ppermute(tail, axis, [(i, (i + 1) % count) for i in range(ends)]),
                cells,
                lax.ppermute(head, axis, [((i + 1) % count, i) for i in range(ends)]),
            ],
            axis=dim,
        )
    return cells


def exchange_faces(v):
    return extended(v, (("flow", 0),), 1)


def operate(v, tiles, scale, storage, cond_all):
    padded = exchange_faces(v)
    local = jnp.einsum("bij,bj->bi", tiles, scale * v, precision=lax.Precision.HIGHEST) * scale
    cond = cond_all[1:]
    cprv = cond_all[:-1]
    return storage * v + local + (cond + cprv) * v - cond * padded[2:] - cprv * padded[:-2]


def squares(residual):
    return lax.psum(jnp.sum(residual * residual), "flow")


def curving(direction, image):
    return lax.psum(jnp.sum(direction * image), "flow")


def solve_flow(source, tiles, scale, storage, cond_all):
    pressure = jnp.zeros_like(source)
    residual = source
    direction = source
    norm_now = squares(residual)
    for step in range(CG):
        image = operate(direction, tiles, scale, storage, cond_all)
        alpha = norm_now / curving(direction, image)
        pressure = pressure + alpha * direction
        residual = residual - alpha * image
        norm_next = squares(residual)
        direction = residual + norm_next / norm_now * direction
        norm_now = norm_next
    return pressure


def plain(source, aperture_rest, storage, geometry, tiles, near, basis_in, core, basis_out):
    blocks, width = source.shape
    groups = lax.axis_size("mech")
    owner = lax.axis_index("mech")
    clusters = near.shape[0]
    span = near.shape[2]
    aperture = aperture_rest
    stacked = jnp.stack([aperture, geometry])
    padded = extended(stacked, (("flow", 1),), 1)
    ap_pad = padded[0]
    geo_pad = padded[1]
    cond_all = geo_pad[:-1] * (ap_pad[:-1] ** 3 + ap_pad[1:] ** 3) * 0.5
    scale = aperture**1.5
    pressure = solve_flow(source, tiles, scale, storage, cond_all)
    packed = pressure.astype(jnp.bfloat16).reshape(clusters, span * groups)
    piece = lax.dynamic_slice_in_dim(packed, owner * span, span, 1)
    partial_value = jnp.einsum(
        "cij,cj->ci", near, piece, preferred_element_type=jnp.float32
    ).reshape(blocks, width)
    coeffs = lax.psum(
        jnp.dot(pressure.reshape(-1), basis_in, precision=lax.Precision.HIGHEST), "flow"
    )
    mixed = jnp.dot(core, coeffs, precision=lax.Precision.HIGHEST)
    near_disp = lax.psum(partial_value, "mech")
    far_disp = jnp.dot(basis_out, mixed, precision=lax.Precision.HIGHEST).reshape(blocks, width)
    aperture = aperture_rest * (1.0 + 0.5 * jnp.tanh(near_disp + far_disp))
    return (pressure, aperture)


def tile_group(weights, u, g, count=8):
    hi, lo = split(u)
    left = jnp.concatenate(
        [jnp.concatenate([hi, hi], 1), jnp.concatenate([lo, jnp.zeros_like(lo)], 1)], 0
    )
    out = jnp.dot(left, weights[g, :, 0 : count * 128], preferred_element_type=F32)
    rows = [
        out[k : k + 1, k * 128 : k * 128 + 128] + out[8 + k : 9 + k, k * 128 : k * 128 + 128]
        for k in range(count)
    ]
    return jnp.concatenate(rows, axis=0)


def closing(p_in, shift, rest, p_out, a_out):
    p_out[...] = p_in[...]
    a_out[...] = rest[...] * (1.0 + 0.5 * jnp.tanh(shift[...]))


def kernel(
    nf, nm, blocks,
    src_h, ap_h, st_h, ge_h, tiles_h, near_h, bin_h, core_h, bout_h,
    p_h, a_h, f_h,
    ext, tiles, ghost, weights, near, bin_v, core, bout,
    vec, img, diag, cnext, cprev, scale, p_v, a_v, f_v, far, rows,
    m1, m2, m3, mz,
    lsem, tsem, osem, xsem, bsem, zsem,
):
    me = lax.axis_index("flow")
    owner = lax.axis_index("mech")
    right = lax.rem(me + 1, nf)
    left = lax.rem(me + nf - 1, nf)
    head = me == 0
    tail = me == nf - 1
    groups = blocks // 8
    chunk = blocks // 4
    last = blocks - 1
    own = slice(8, 8 + blocks)
    wide = blocks + 16
    body = slice(8, 8 + wide)
    above = slice(7, 7 + wide)
    below = slice(9, 9 + wide)
    mid = slice(16, 16 + blocks)
    zero_row = jnp.zeros((1, 128), F32)

    loads = []

    def load(i, a, b):
        c = pltpu.make_async_copy(a, b, lsem.at[i])
        c.start()
        loads.append(c)

    for i, ref in enumerate((src_h, ap_h, ge_h, st_h)):
        load(i, ref, ext.at[i, pl.ds(8, blocks)])
    tloads = []
    for q in range(4):
        part = pl.ds(q * chunk, chunk)
        c = pltpu.make_async_copy(tiles_h.at[part], tiles.at[part], tsem.at[q])
        c.start()
        tloads.append(c)

    barrier = pltpu.get_barrier_semaphore()

    def greet(d, carry):
        pl.semaphore_signal(
            barrier, inc=1, device_id={"flow": lax.rem(me + d, nf)}, device_id_type=MESH
        )
        return carry

    lax.fori_loop(1, nf, greet, 0)
    for d in range(1, nm):
        pl.semaphore_signal(
            barrier, inc=1, device_id={"mech": lax.rem(owner + d, nm)}, device_id_type=MESH
        )

    def spread(buf, i, size):
        mine = buf.at[pl.ds(pl.multiple_of(me * 8, 8), size)]

        def one(d, carry):
            pltpu.make_async_remote_copy(
                src_ref=mine,
                dst_ref=mine,
                send_sem=bsem.at[i, 0],
                recv_sem=bsem.at[i, 1],
                device_id={"flow": lax.rem(me + d, nf)},
                device_id_type=MESH,
            ).start()
            return carry

        lax.fori_loop(1, nf, one, 0)

    def gather_wait(buf, i, which, size):
        others = buf.at[pl.ds(0, (nf - 1) * size)]
        pltpu.make_async_copy(others, others, bsem.at[i, which]).wait()

    def slots(buf, row):
        return buf[pl.ds(row, nf, stride=8), :]

    def spot():
        return pl.ds(pl.multiple_of(me * 8, 8), 8)

    def dot_row(i, x, y):
        rows[i : i + 1, :] = jnp.sum(x * y, axis=0, keepdims=True)

    def row_sums():
        sums = jnp.sum(rows[...].T, axis=0, keepdims=True)
        return jnp.concatenate([sums, jnp.zeros((1, 96), F32)], axis=1)

    def lane(row, i):
        return jnp.broadcast_to(row[:, i : i + 1], (1, 128))

    def total_of(x):
        x = jnp.sum(x, axis=0, keepdims=True)
        return jnp.broadcast_to(jnp.sum(x, axis=1, keepdims=True), (1, 128))

    rows[...] = jnp.zeros_like(rows)
    m1[pl.ds(nf * 8, 8), :] = jnp.zeros((8, 128), F32)
    m2[pl.ds(nf * 8, 8), :] = jnp.zeros((8, 128), F32)
    for k in range(NV):
        vec[k, 0:8, :] = jnp.zeros((8, 128), F32)
        vec[k, 8 + wide : 16 + wide, :] = jnp.zeros((8, 128), F32)
        img[k, 0:8, :] = jnp.zeros((8, 128), F32)
        img[k, 8 + blocks : wide, :] = jnp.zeros((8, 128), F32)

    for i in range(3):
        loads[i].wait()
    a = ext[1, own, :]
    b = ext[0, own, :]
    s = a * jnp.sqrt(a)
    scale[own, :] = s

    def prepare(tile, g, k):
        hi, lo = split(tile)
        weights[g, 0:128, k * 128 : k * 128 + 128] = hi
        weights[g, 128:256, k * 128 : k * 128 + 128] = lo

    for q in range(4):
        tloads[q].wait()
        for g in range(q * groups // 4, (q + 1) * groups // 4):
            for k in range(8):
                prepare(tiles[g * 8 + k], g, k)
            part = slice(8 + g * 8, 16 + g * 8)
            ext[4, part, :] = tile_group(weights, scale[part, :] * ext[0, part, :], g)

    load(4, bin_h, bin_v)
    load(5, near_h, near)
    load(6, core_h, core)
    load(7, bout_h, bout)
    loads[3].wait()
    cube = a * a * a
    half = ext[2, own, :] * 0.5
    edge = half[last:] * cube[last:]
    inner = half[:last] * (cube[:last] + cube[1:])
    cond = jnp.concatenate([inner, jnp.where(tail, edge, zero_row)], axis=0)
    cp = jnp.concatenate([zero_row, inner], axis=0)
    ahead = jnp.concatenate([b[1:], zero_row], axis=0)
    behind = jnp.concatenate([zero_row, b[:last]], axis=0)
    alone = (ext[3, own, :] + cond + cp) * b + s * ext[4, own, :] - cond * ahead - cp * behind
    img[0, own, :] = alone
    for g in (0, groups - 1):
        part = slice(8 + g * 8, 16 + g * 8)
        ext[5, part, :] = tile_group(weights, scale[part, :] * img[0, part, :], g)
    dot_row(0, b, b)
    dot_row(1, b, alone)
    dot_row(2, alone, alone)
    rows[3:4, :] = jnp.where(tail, zero_row, half[last:]) * (1.0 / 128.0)
    rows[4:5, :] = cube[last:] * (1.0 / 128.0)
    rows[5:6, :] = cube[0:1] * (1.0 / 128.0)
    m1[spot(), :] = jnp.concatenate(
        [row_sums(), b[last:], b[0:1], jnp.zeros((5, 128), F32)], axis=0
    )
    pl.semaphore_wait(barrier, nf - 1 + nm - 1)

    pending = []

    def hand_over(a, b, i, dev):
        c = pltpu.make_async_remote_copy(
            src_ref=a, dst_ref=b, send_sem=xsem.at[i, 0], recv_sem=xsem.at[i, 1],
            device_id={"flow": dev}, device_id_type=MESH,
        )
        c.start()
        pending.append(c)

    hand_over(ext.at[:, pl.ds(blocks, 8)], ext.at[:, pl.ds(0, 8)], 0, right)
    hand_over(ext.at[:, pl.ds(8, 8)], ext.at[:, pl.ds(8 + blocks, 8)], 1, left)
    spread(m1, 0, 3)
    hand_over(tiles.at[blocks - 1], ghost.at[0], 2, right)
    hand_over(tiles.at[0], ghost.at[1], 3, left)
    pending[0].wait_recv()
    pending[1].wait_recv()

    row = lax.broadcasted_iota(jnp.int32, (wide, 128), 0)
    at_tail = row == jnp.where(tail, 7 + blocks, -1)
    at_head = row == jnp.where(head, 7, -1)
    a = ext[1]
    s = a * jnp.sqrt(a)
    scale[...] = s
    cube = a * a * a
    cube_next = jnp.where(at_tail, 0.0, jnp.concatenate([cube[1:], zero_row], axis=0))
    cond = jnp.where(at_head, 0.0, ext[2] * (cube + cube_next) * 0.5)
    cp = jnp.concatenate([zero_row, cond[:-1]], axis=0)
    cnext[...] = jnp.where(at_tail, 0.0, cond)
    cprev[...] = cp
    diag[...] = ext[3] + cond + cp
    vec[0, body, :] = ext[0]
    img[0] = ext[4]

    def finish(k):
        img[k] = (
            diag[...] * vec[k, body, :]
            + scale[...] * img[k]
            - cnext[...] * vec[k, below, :]
            - cprev[...] * vec[k, above, :]
        )

    def product(k):
        for g in range(groups):
            part = slice(8 + g * 8, 16 + g * 8)
            u = scale[part, :] * vec[k, 16 + g * 8 : 24 + g * 8, :]
            img[k, part, :] = tile_group(weights, u, g)

    def ghost_product(k):
        low, high = slice(7, 8), slice(8 + blocks, 9 + blocks)
        u = jnp.concatenate(
            [
                scale[low, :] * vec[k, 15:16, :],
                scale[high, :] * vec[k, 16 + blocks : 17 + blocks, :],
                jnp.zeros((6, 128), F32),
            ],
            axis=0,
        )
        out = tile_group(weights, u, groups, 2)
        img[k, low, :] = out[0:1]
        img[k, high, :] = out[1:2]

    finish(0)
    vec[1, body, :] = img[0]
    product(1)
    pending[2].wait_recv()
    pending[3].wait_recv()
    for k in range(2):
        prepare(ghost[k], groups, k)
    ghost_product(1)
    img[1, 6:7, :] = ext[5, 6:7, :]
    img[1, 9 + blocks : 10 + blocks, :] = ext[5, 9 + blocks : 10 + blocks, :]
    finish(1)
    gather_wait(m1, 0, 1, 3)

    def following(row):
        return m1[pl.ds(8 + row, nf, stride=8), :]

    sums = slots(m1, 0)
    total = jnp.sum(sums, axis=0, keepdims=True)
    gap = slots(m1, 1) - following(2)
    flux = sums[:, 3:4] * (sums[:, 4:5] + following(0)[:, 5:6]) * gap
    bb = lane(total, 0)
    bw = lane(total, 1) + total_of(flux * gap)
    ww = lane(total, 2) + 2.0 * total_of(flux * (lane(total, 1) / bb * gap + flux))
    mean = bw / bb
    dev = jnp.sqrt(jnp.maximum(ww / bb - mean * mean, (0.01 * mean) * (0.01 * mean)))
    inv = 1.0 / dev
    shifted = (mean + 0.8 * dev) * inv
    w0 = img[0]
    b = ext[0]
    v1 = (w0 - mean * b) * inv
    w1 = (img[1] - mean * w0) * inv
    vec[1, body, :] = v1
    img[1] = w1
    vec[2, body, :] = w1 * inv - shifted * v1 - b
    pairs = {}

    def entry(j, k):
        pairs[(j, k)] = len(pairs)
        dot_row(pairs[(j, k)], vec[k, mid, :], img[j, own, :])

    def against(k):
        pairs[("g", k)] = len(pairs)
        dot_row(pairs[("g", k)], vec[k, mid, :], vec[1, mid, :])

    product(2)
    ghost_product(2)
    for j, k in ((0, 0), (0, 1), (1, 1), (0, 2), (1, 2)):
        entry(j, k)
    for k in range(3):
        against(k)
    finish(2)
    vec[3, body, :] = img[2] * inv - shifted * vec[2, body, :] - vec[1, body, :]
    product(3)
    for j, k in ((2, 2), (0, 3), (1, 3), (2, 3)):
        entry(j, k)
    against(3)
    finish(3)
    vec[4, mid, :] = (
        img[3, own, :] * inv - shifted * vec[3, mid, :] - vec[2, mid, :]
    )
    vec[4, 8:16, :] = jnp.zeros((8, 128), F32)
    vec[4, 16 + blocks : 24 + blocks, :] = jnp.zeros((8, 128), F32)
    product(4)
    for j, k in ((3, 3), (0, 4), (1, 4), (2, 4), (3, 4)):
        entry(j, k)
    against(4)
    finish(4)
    entry(4, 4)
    m2[spot(), :] = jnp.concatenate(
        [
            row_sums(),
            cnext[7 + blocks : 8 + blocks, :] * vec[4, 15 + blocks : 16 + blocks, :],
            vec[4, 16:17, :],
            jnp.zeros((5, 128), F32),
        ],
        axis=0,
    )
    spread(m2, 1, 3)
    loads[4].wait()
    loads[5].wait()
    accs = [jnp.zeros((64, 128), F32)] * NV
    for g in range(blocks):
        cut = bin_v[:, g * 128 : g * 128 + 128]
        accs = [accs[k] + cut * vec[k, 16 + g : 17 + g, :] for k in range(NV)]
    far_rows = [jnp.sum(acc.T, axis=0, keepdims=True) for acc in accs] + [zero_row[:, 0:64]]
    m3[spot(), :] = jnp.concatenate(
        [jnp.concatenate(far_rows[i : i + 2], axis=1) for i in (0, 2, 4)]
        + [jnp.zeros((5, 128), F32)],
        axis=0,
    )
    spread(m3, 2, 3)
    gather_wait(m2, 1, 1, 3)

    total = jnp.sum(slots(m2, 0), axis=0, keepdims=True)
    cross = total_of(slots(m2, 1) * m2[pl.ds(8 + 2, nf, stride=8), :])
    full = [[None] * NV for _ in range(NV)]
    for j in range(NV):
        for k in range(j, NV):
            full[j][k] = lane(total, pairs[(j, k)])
    full[4][4] = full[4][4] - 2.0 * cross
    size = [full[j][j] for j in range(NV)]
    ratio = -dev / mean
    y = [ratio * lane(total, pairs[("g", k)]) for k in range(NV)]
    low = [[None] * NV for _ in range(NV)]
    pivot = [None] * NV
    least = None
    for j in range(NV):
        pivot[j] = 1.0 / full[j][j]
        margin = full[j][j] - LEAST * size[j]
        least = margin if j == 0 else jnp.minimum(least, margin)
        for i in range(j + 1, NV):
            low[i][j] = full[j][i] * pivot[j]
        for i in range(j + 1, NV):
            for k in range(i, NV):
                full[i][k] = full[i][k] - low[i][j] * full[j][k]
            y[i] = y[i] - low[i][j] * y[j]
    coef = [y[j] * pivot[j] for j in range(NV)]
    for j in range(NV - 2, -1, -1):
        for i in range(j + 1, NV):
            coef[j] = coef[j] - low[i][j] * coef[i]
    coef[0] = coef[0] + 1.0 / mean
    p = coef[0] * vec[0, mid, :]
    for k in range(1, NV):
        p = p + coef[k] * vec[k, mid, :]
    p_v[...] = p
    f_h[0, 0] = least[0, 0]
    p_h[...] = p

    clusters = blocks // nm
    mine = jnp.zeros((clusters, 128), F32)
    for q in range(nm):
        mine = jnp.where(owner == q, p_v[pl.ds(q, clusters, stride=nm), :], mine)
    mine = mine.astype(BF16)
    per = clusters // 4
    for r in range(4):
        for c in range(r * per, (r + 1) * per):
            full_c = lax.dot_general(
                mine, near[c], (((1,), (1,)), ((), ())), preferred_element_type=F32
            )
            for q in range(nm):
                mz[owner, nm * c + q : nm * c + q + 1, :] = full_c[
                    c : c + 1, q * 128 : q * 128 + 128
                ]
        piece = mz.at[owner, pl.ds(r * per * nm, per * nm)]
        for d in range(1, nm):
            pltpu.make_async_remote_copy(
                src_ref=piece,
                dst_ref=piece,
                send_sem=zsem.at[r, 0],
                recv_sem=zsem.at[r, 1],
                device_id={"mech": lax.rem(owner + d, nm)},
                device_id_type=MESH,
            ).start()
    def z_wait(r, which):
        others = mz.at[pl.ds(0, nm - 1), pl.ds(r * per * nm, per * nm)]
        pltpu.make_async_copy(others, others, zsem.at[r, which]).wait()

    loads[6].wait()
    loads[7].wait()
    gather_wait(m3, 2, 1, 3)
    lower = lax.broadcasted_iota(jnp.int32, (1, 128), 1) < 64
    parts = [jnp.sum(slots(m3, i), axis=0, keepdims=True) for i in range(3)]
    both = (
        jnp.where(lower, coef[0], coef[1]) * parts[0]
        + jnp.where(lower, coef[2], coef[3]) * parts[1]
        + coef[4] * parts[2]
    )
    coeffs = both[:, 0:64] + both[:, 64:128]
    mixed = jnp.sum(core[...] * coeffs, axis=1, keepdims=True)
    mixed = jnp.broadcast_to(mixed, (64, 128))
    for g in range(blocks):
        far[g : g + 1, :] = jnp.sum(
            bout[:, g * 128 : g * 128 + 128] * mixed, axis=0, keepdims=True
        )
    for r in range(4):
        z_wait(r, 1)
    a_h[...] = jnp.sum(mz[...], axis=0) + far[...]
    for c in pending:
        c.wait_send()
    gather_wait(m1, 0, 0, 3)
    gather_wait(m2, 1, 0, 3)
    gather_wait(m3, 2, 0, 3)
    for r in range(4):
        z_wait(r, 0)


def solution(mesh):
    nf = mesh.shape["flow"]
    nm = mesh.shape["mech"]

    def local(source, aperture_rest, storage, geometry, tiles, near, basis_in, core, basis_out):
        blocks, width = source.shape
        rank = core.shape[0]
        grid = (blocks, width)
        vm = pltpu.VMEM
        wide = (blocks + 16, width)
        scratch = [
            vm((6,) + wide, F32), vm(tiles.shape, F32), vm((2, width, width), F32),
            vm((blocks // 8 + 1, 2 * width, 8 * width), BF16),
            vm(near.shape, BF16), vm((rank, basis_in.shape[0]), F32), vm(core.shape, F32),
            vm((rank, basis_in.shape[0]), F32),
            vm((NV, blocks + 32, width), F32), vm((NV,) + wide, F32),
            vm(wide, F32), vm(wide, F32), vm(wide, F32), vm(wide, F32),
            vm(grid, F32), vm(grid, F32), vm((8, width), F32), vm(grid, F32), vm((32, width), F32),
            vm(((nf + 1) * 8, width), F32), vm(((nf + 1) * 8, width), F32),
            vm((nf * 8, width), F32), vm((nm,) + grid, F32),
            pltpu.SemaphoreType.DMA((8,)), pltpu.SemaphoreType.DMA((4,)),
            pltpu.SemaphoreType.DMA((3,)), pltpu.SemaphoreType.DMA((4, 2)),
            pltpu.SemaphoreType.DMA((3, 2)), pltpu.SemaphoreType.DMA((4, 2)),
        ]
        anywhere = pl.BlockSpec(memory_space=pltpu.HBM)
        pressure, shift, margin = pl.pallas_call(
            functools.partial(kernel, nf, nm, blocks),
            out_shape=(
                jax.ShapeDtypeStruct(grid, F32),
                jax.ShapeDtypeStruct(grid, F32),
                jax.ShapeDtypeStruct((1, 1), F32),
            ),
            in_specs=[anywhere] * 9,
            out_specs=(
                pl.BlockSpec(memory_space=pltpu.VMEM),
                pl.BlockSpec(memory_space=pltpu.VMEM),
                pl.BlockSpec(memory_space=pltpu.SMEM),
            ),
            scratch_shapes=scratch,
            compiler_params=pltpu.CompilerParams(
                collective_id=0, has_side_effects=True, vmem_limit_bytes=63 << 20
            ),
        )(
            source, aperture_rest, storage, geometry, tiles, near,
            basis_in.T, core, basis_out.T,
        )
        end = pl.pallas_call(
            closing,
            out_shape=(jax.ShapeDtypeStruct(grid, F32), jax.ShapeDtypeStruct(grid, F32)),
            in_specs=[pl.BlockSpec(memory_space=pltpu.VMEM)] * 3,
            out_specs=(pl.BlockSpec(memory_space=pltpu.VMEM),) * 2,
        )
        return lax.cond(
            margin[0, 0] > 0.0,
            lambda: end(pressure, shift, aperture_rest),
            lambda: plain(
                source, aperture_rest, storage, geometry, tiles, near, basis_in, core, basis_out
            ),
        )

    placed = (
        P("flow", None), P("flow", None), P("flow", None), P("flow", None),
        P("flow", None, None), P("flow", None, "mech"), P("flow", None), P(), P("flow", None),
    )
    return jax.shard_map(
        local,
        mesh=mesh,
        in_specs=placed,
        out_specs=(P("flow", None), P("flow", None)),
        check_vma=False,
    )
```

```python
import functools
import jax
import jax.numpy as jnp
from jax import lax
from jax.experimental import pallas as pl
from jax.experimental.pallas import tpu as pltpu
from jax.sharding import PartitionSpec as P

F32 = jnp.float32
BF16 = jnp.bfloat16
MESH = pl.DeviceIdType.MESH
NV = 5
LEAST = 3e-3


def split(x):
    hi = x.astype(BF16)
    return hi, (x - hi.astype(F32)).astype(BF16)


CG = 5


def extended(cells, sides, width):
    for axis, dim in sides:
        count = lax.axis_size(axis)
        ends = count - 1
        head = lax.slice_in_dim(cells, 0, width, axis=dim)
        tail = lax.slice_in_dim(cells, cells.shape[dim] - width, cells.shape[dim], axis=dim)
        cells = jnp.concatenate(
            [
                lax.ppermute(tail, axis, [(i, (i + 1) % count) for i in range(ends)]),
                cells,
                lax.ppermute(head, axis, [((i + 1) % count, i) for i in range(ends)]),
            ],
            axis=dim,
        )
    return cells


def exchange_faces(v):
    return extended(v, (("flow", 0),), 1)


def operate(v, tiles, scale, storage, cond_all):
    padded = exchange_faces(v)
    local = jnp.einsum("bij,bj->bi", tiles, scale * v, precision=lax.Precision.HIGHEST) * scale
    cond = cond_all[1:]
    cprv = cond_all[:-1]
    return storage * v + local + (cond + cprv) * v - cond * padded[2:] - cprv * padded[:-2]


def squares(residual):
    return lax.psum(jnp.sum(residual * residual), "flow")


def curving(direction, image):
    return lax.psum(jnp.sum(direction * image), "flow")


def solve_flow(source, tiles, scale, storage, cond_all):
    pressure = jnp.zeros_like(source)
    residual = source
    direction = source
    norm_now = squares(residual)
    for step in range(CG):
        image = operate(direction, tiles, scale, storage, cond_all)
        alpha = norm_now / curving(direction, image)
        pressure = pressure + alpha * direction
        residual = residual - alpha * image
        norm_next = squares(residual)
        direction = residual + norm_next / norm_now * direction
        norm_now = norm_next
    return pressure


def plain(source, aperture_rest, storage, geometry, tiles, near, basis_in, core, basis_out):
    blocks, width = source.shape
    groups = lax.axis_size("mech")
    owner = lax.axis_index("mech")
    clusters = near.shape[0]
    span = near.shape[2]
    aperture = aperture_rest
    stacked = jnp.stack([aperture, geometry])
    padded = extended(stacked, (("flow", 1),), 1)
    ap_pad = padded[0]
    geo_pad = padded[1]
    cond_all = geo_pad[:-1] * (ap_pad[:-1] ** 3 + ap_pad[1:] ** 3) * 0.5
    scale = aperture**1.5
    pressure = solve_flow(source, tiles, scale, storage, cond_all)
    packed = pressure.astype(jnp.bfloat16).reshape(clusters, span * groups)
    piece = lax.dynamic_slice_in_dim(packed, owner * span, span, 1)
    partial_value = jnp.einsum(
        "cij,cj->ci", near, piece, preferred_element_type=jnp.float32
    ).reshape(blocks, width)
    coeffs = lax.psum(
        jnp.dot(pressure.reshape(-1), basis_in, precision=lax.Precision.HIGHEST), "flow"
    )
    mixed = jnp.dot(core, coeffs, precision=lax.Precision.HIGHEST)
    near_disp = lax.psum(partial_value, "mech")
    far_disp = jnp.dot(basis_out, mixed, precision=lax.Precision.HIGHEST).reshape(blocks, width)
    aperture = aperture_rest * (1.0 + 0.5 * jnp.tanh(near_disp + far_disp))
    return (pressure, aperture)


def tile_group(weights, u, g, count=8):
    hi, lo = split(u)
    left = jnp.concatenate(
        [jnp.concatenate([hi, hi], 1), jnp.concatenate([lo, jnp.zeros_like(lo)], 1)], 0
    )
    out = jnp.dot(left, weights[g, :, 0 : count * 128], preferred_element_type=F32)
    rows = [
        out[k : k + 1, k * 128 : k * 128 + 128] + out[8 + k : 9 + k, k * 128 : k * 128 + 128]
        for k in range(count)
    ]
    return jnp.concatenate(rows, axis=0)


def closing(p_in, shift, rest, p_out, a_out):
    p_out[...] = p_in[...]
    a_out[...] = rest[...] * (1.0 + 0.5 * jnp.tanh(shift[...]))


def kernel(
    nf, nm, blocks,
    src_h, ap_h, st_h, ge_h, tiles_h, near_h, bin_h, core_h, bout_h,
    p_h, a_h, f_h,
    ext, tiles, ghost, weights, near, bin_v, core, bout,
    vec, img, diag, cnext, cprev, scale, p_v, far, rows,
    m1, m2, m3, mz,
    lsem, tsem, xsem, bsem, zsem,
):
    me = lax.axis_index("flow")
    owner = lax.axis_index("mech")
    right = lax.rem(me + 1, nf)
    left = lax.rem(me + nf - 1, nf)
    head = me == 0
    tail = me == nf - 1
    groups = blocks // 8
    chunk = blocks // 4
    last = blocks - 1
    own = slice(8, 8 + blocks)
    wide = blocks + 16
    body = slice(8, 8 + wide)
    above = slice(7, 7 + wide)
    below = slice(9, 9 + wide)
    mid = slice(16, 16 + blocks)
    zero_row = jnp.zeros((1, 128), F32)

    loads = []

    def load(i, a, b):
        c = pltpu.make_async_copy(a, b, lsem.at[i])
        c.start()
        loads.append(c)

    for i, ref in enumerate((src_h, ap_h, ge_h, st_h)):
        load(i, ref, ext.at[i, pl.ds(8, blocks)])
    tloads = []
    for q in range(4):
        part = pl.ds(q * chunk, chunk)
        c = pltpu.make_async_copy(tiles_h.at[part], tiles.at[part], tsem.at[q])
        c.start()
        tloads.append(c)

    barrier = pltpu.get_barrier_semaphore()

    def greet(d, carry):
        pl.semaphore_signal(
            barrier, inc=1, device_id={"flow": lax.rem(me + d, nf)}, device_id_type=MESH
        )
        return carry

    lax.fori_loop(1, nf, greet, 0)
    for d in range(1, nm):
        pl.semaphore_signal(
            barrier, inc=1, device_id={"mech": lax.rem(owner + d, nm)}, device_id_type=MESH
        )

    def spread(buf, i, size):
        mine = buf.at[pl.ds(pl.multiple_of(me * 8, 8), size)]

        def one(d, carry):
            pltpu.make_async_remote_copy(
                src_ref=mine,
                dst_ref=mine,
                send_sem=bsem.at[i, 0],
                recv_sem=bsem.at[i, 1],
                device_id={"flow": lax.rem(me + d, nf)},
                device_id_type=MESH,
            ).start()
            return carry

        lax.fori_loop(1, nf, one, 0)

    def gather_wait(buf, i, which, size):
        others = buf.at[pl.ds(0, (nf - 1) * size)]
        pltpu.make_async_copy(others, others, bsem.at[i, which]).wait()

    def slots(buf, row):
        return buf[pl.ds(row, nf, stride=8), :]

    def spot():
        return pl.ds(pl.multiple_of(me * 8, 8), 8)

    def dot_row(i, x, y):
        rows[i : i + 1, :] = jnp.sum(x * y, axis=0, keepdims=True)

    def row_sums():
        sums = jnp.sum(rows[...].T, axis=0, keepdims=True)
        return jnp.concatenate([sums, jnp.zeros((1, 96), F32)], axis=1)

    def lane(row, i):
        return jnp.broadcast_to(row[:, i : i + 1], (1, 128))

    def total_of(x):
        x = jnp.sum(x, axis=0, keepdims=True)
        return jnp.broadcast_to(jnp.sum(x, axis=1, keepdims=True), (1, 128))

    rows[...] = jnp.zeros_like(rows)
    m1[pl.ds(nf * 8, 8), :] = jnp.zeros((8, 128), F32)
    m2[pl.ds(nf * 8, 8), :] = jnp.zeros((8, 128), F32)
    for k in range(NV):
        vec[k, 0:8, :] = jnp.zeros((8, 128), F32)
        vec[k, 8 + wide : 16 + wide, :] = jnp.zeros((8, 128), F32)
        img[k, 0:8, :] = jnp.zeros((8, 128), F32)
        img[k, 8 + blocks : wide, :] = jnp.zeros((8, 128), F32)

    for i in range(3):
        loads[i].wait()
    a = ext[1, own, :]
    b = ext[0, own, :]
    s = a * jnp.sqrt(a)
    scale[own, :] = s

    def prepare(tile, g, k):
        hi, lo = split(tile)
        weights[g, 0:128, k * 128 : k * 128 + 128] = hi
        weights[g, 128:256, k * 128 : k * 128 + 128] = lo

    for q in range(4):
        tloads[q].wait()
        for g in range(q * groups // 4, (q + 1) * groups // 4):
            for k in range(8):
                prepare(tiles[g * 8 + k], g, k)
            part = slice(8 + g * 8, 16 + g * 8)
            ext[4, part, :] = tile_group(weights, scale[part, :] * ext[0, part, :], g)

    load(4, bin_h, bin_v)
    load(5, near_h, near)
    load(6, core_h, core)
    load(7, bout_h, bout)
    loads[3].wait()
    cube = a * a * a
    half = ext[2, own, :] * 0.5
    edge = half[last:] * cube[last:]
    inner = half[:last] * (cube[:last] + cube[1:])
    cond = jnp.concatenate([inner, jnp.where(tail, edge, zero_row)], axis=0)
    cp = jnp.concatenate([zero_row, inner], axis=0)
    ahead = jnp.concatenate([b[1:], zero_row], axis=0)
    behind = jnp.concatenate([zero_row, b[:last]], axis=0)
    alone = (ext[3, own, :] + cond + cp) * b + s * ext[4, own, :] - cond * ahead - cp * behind
    img[0, own, :] = alone
    for g in (0, groups - 1):
        part = slice(8 + g * 8, 16 + g * 8)
        ext[5, part, :] = tile_group(weights, scale[part, :] * img[0, part, :], g)
    dot_row(0, b, b)
    dot_row(1, b, alone)
    dot_row(2, alone, alone)
    rows[3:4, :] = jnp.where(tail, zero_row, half[last:]) * (1.0 / 128.0)
    rows[4:5, :] = cube[last:] * (1.0 / 128.0)
    rows[5:6, :] = cube[0:1] * (1.0 / 128.0)
    m1[spot(), :] = jnp.concatenate(
        [row_sums(), b[last:], b[0:1], jnp.zeros((5, 128), F32)], axis=0
    )
    pl.semaphore_wait(barrier, nf - 1 + nm - 1)

    pending = []

    def hand_over(a, b, i, dev):
        c = pltpu.make_async_remote_copy(
            src_ref=a, dst_ref=b, send_sem=xsem.at[i, 0], recv_sem=xsem.at[i, 1],
            device_id={"flow": dev}, device_id_type=MESH,
        )
        c.start()
        pending.append(c)

    hand_over(ext.at[:, pl.ds(blocks, 8)], ext.at[:, pl.ds(0, 8)], 0, right)
    hand_over(ext.at[:, pl.ds(8, 8)], ext.at[:, pl.ds(8 + blocks, 8)], 1, left)
    spread(m1, 0, 3)
    hand_over(tiles.at[blocks - 1], ghost.at[0], 2, right)
    hand_over(tiles.at[0], ghost.at[1], 3, left)
    pending[0].wait_recv()
    pending[1].wait_recv()

    row = lax.broadcasted_iota(jnp.int32, (wide, 128), 0)
    at_tail = row == jnp.where(tail, 7 + blocks, -1)
    at_head = row == jnp.where(head, 7, -1)
    a = ext[1]
    s = a * jnp.sqrt(a)
    scale[...] = s
    cube = a * a * a
    cube_next = jnp.where(at_tail, 0.0, jnp.concatenate([cube[1:], zero_row], axis=0))
    cond = jnp.where(at_head, 0.0, ext[2] * (cube + cube_next) * 0.5)
    cp = jnp.concatenate([zero_row, cond[:-1]], axis=0)
    cnext[...] = jnp.where(at_tail, 0.0, cond)
    cprev[...] = cp
    diag[...] = ext[3] + cond + cp
    vec[0, body, :] = ext[0]
    img[0] = ext[4]

    def finish(k):
        img[k] = (
            diag[...] * vec[k, body, :]
            + scale[...] * img[k]
            - cnext[...] * vec[k, below, :]
            - cprev[...] * vec[k, above, :]
        )

    def product(k):
        for g in range(groups):
            part = slice(8 + g * 8, 16 + g * 8)
            u = scale[part, :] * vec[k, 16 + g * 8 : 24 + g * 8, :]
            img[k, part, :] = tile_group(weights, u, g)

    def ghost_product(k):
        low, high = slice(7, 8), slice(8 + blocks, 9 + blocks)
        u = jnp.concatenate(
            [
                scale[low, :] * vec[k, 15:16, :],
                scale[high, :] * vec[k, 16 + blocks : 17 + blocks, :],
                jnp.zeros((6, 128), F32),
            ],
            axis=0,
        )
        out = tile_group(weights, u, groups, 2)
        img[k, low, :] = out[0:1]
        img[k, high, :] = out[1:2]

    finish(0)
    vec[1, body, :] = img[0]
    product(1)
    pending[2].wait_recv()
    pending[3].wait_recv()
    for k in range(2):
        prepare(ghost[k], groups, k)
    ghost_product(1)
    img[1, 6:7, :] = ext[5, 6:7, :]
    img[1, 9 + blocks : 10 + blocks, :] = ext[5, 9 + blocks : 10 + blocks, :]
    finish(1)
    gather_wait(m1, 0, 1, 3)

    def following(row):
        return m1[pl.ds(8 + row, nf, stride=8), :]

    sums = slots(m1, 0)
    total = jnp.sum(sums, axis=0, keepdims=True)
    gap = slots(m1, 1) - following(2)
    flux = sums[:, 3:4] * (sums[:, 4:5] + following(0)[:, 5:6]) * gap
    bb = lane(total, 0)
    bw = lane(total, 1) + total_of(flux * gap)
    ww = lane(total, 2) + 2.0 * total_of(flux * (lane(total, 1) / bb * gap + flux))
    mean = bw / bb
    dev = jnp.sqrt(jnp.maximum(ww / bb - mean * mean, (0.01 * mean) * (0.01 * mean)))
    inv = 1.0 / dev
    shifted = (mean + 0.8 * dev) * inv
    w0 = img[0]
    b = ext[0]
    v1 = (w0 - mean * b) * inv
    w1 = (img[1] - mean * w0) * inv
    vec[1, body, :] = v1
    img[1] = w1
    vec[2, body, :] = w1 * inv - shifted * v1 - b
    pairs = {}

    def entry(j, k):
        pairs[(j, k)] = len(pairs)
        dot_row(pairs[(j, k)], vec[k, mid, :], img[j, own, :])

    def against(k):
        pairs[("g", k)] = len(pairs)
        dot_row(pairs[("g", k)], vec[k, mid, :], vec[1, mid, :])

    product(2)
    ghost_product(2)
    for j, k in ((0, 0), (0, 1), (1, 1), (0, 2), (1, 2)):
        entry(j, k)
    for k in range(3):
        against(k)
    finish(2)
    vec[3, body, :] = img[2] * inv - shifted * vec[2, body, :] - vec[1, body, :]
    product(3)
    for j, k in ((2, 2), (0, 3), (1, 3), (2, 3)):
        entry(j, k)
    against(3)
    finish(3)
    vec[4, mid, :] = (
        img[3, own, :] * inv - shifted * vec[3, mid, :] - vec[2, mid, :]
    )
    vec[4, 8:16, :] = jnp.zeros((8, 128), F32)
    vec[4, 16 + blocks : 24 + blocks, :] = jnp.zeros((8, 128), F32)
    product(4)
    for j, k in ((3, 3), (0, 4), (1, 4), (2, 4), (3, 4)):
        entry(j, k)
    against(4)
    finish(4)
    entry(4, 4)
    m2[spot(), :] = jnp.concatenate(
        [
            row_sums(),
            cnext[7 + blocks : 8 + blocks, :] * vec[4, 15 + blocks : 16 + blocks, :],
            vec[4, 16:17, :],
            jnp.zeros((5, 128), F32),
        ],
        axis=0,
    )
    spread(m2, 1, 3)
    loads[4].wait()
    loads[5].wait()
    accs = [jnp.zeros((64, 128), F32)] * NV
    for g in range(blocks):
        cut = bin_v[:, g * 128 : g * 128 + 128]
        accs = [accs[k] + cut * vec[k, 16 + g : 17 + g, :] for k in range(NV)]
    far_rows = [jnp.sum(acc.T, axis=0, keepdims=True) for acc in accs] + [zero_row[:, 0:64]]
    m3[spot(), :] = jnp.concatenate(
        [jnp.concatenate(far_rows[i : i + 2], axis=1) for i in (0, 2, 4)]
        + [jnp.zeros((5, 128), F32)],
        axis=0,
    )
    spread(m3, 2, 3)
    gather_wait(m2, 1, 1, 3)

    total = jnp.sum(slots(m2, 0), axis=0, keepdims=True)
    cross = total_of(slots(m2, 1) * m2[pl.ds(8 + 2, nf, stride=8), :])
    full = [[None] * NV for _ in range(NV)]
    for j in range(NV):
        for k in range(j, NV):
            full[j][k] = lane(total, pairs[(j, k)])
    full[4][4] = full[4][4] - 2.0 * cross
    size = [full[j][j] for j in range(NV)]
    ratio = -dev / mean
    y = [ratio * lane(total, pairs[("g", k)]) for k in range(NV)]
    low = [[None] * NV for _ in range(NV)]
    pivot = [None] * NV
    least = None
    for j in range(NV):
        pivot[j] = 1.0 / full[j][j]
        margin = full[j][j] - LEAST * size[j]
        least = margin if j == 0 else jnp.minimum(least, margin)
        for i in range(j + 1, NV):
            low[i][j] = full[j][i] * pivot[j]
        for i in range(j + 1, NV):
            for k in range(i, NV):
                full[i][k] = full[i][k] - low[i][j] * full[j][k]
            y[i] = y[i] - low[i][j] * y[j]
    coef = [y[j] * pivot[j] for j in range(NV)]
    for j in range(NV - 2, -1, -1):
        for i in range(j + 1, NV):
            coef[j] = coef[j] - low[i][j] * coef[i]
    coef[0] = coef[0] + 1.0 / mean
    p = coef[0] * vec[0, mid, :]
    for k in range(1, NV):
        p = p + coef[k] * vec[k, mid, :]
    p_v[0:blocks, :] = p
    f_h[0, 0] = least[0, 0]
    p_h[...] = p

    clusters = blocks // nm
    mine = jnp.zeros((clusters, 128), F32)
    for q in range(nm):
        mine = jnp.where(owner == q, p_v[pl.ds(q, clusters, stride=nm), :], mine)
    mine = mine.astype(BF16)
    per = clusters // 4
    for r in range(4):
        for c in range(r * per, (r + 1) * per):
            full_c = lax.dot_general(
                mine, near[c], (((1,), (1,)), ((), ())), preferred_element_type=F32
            )
            for q in range(nm):
                mz[owner, nm * c + q : nm * c + q + 1, :] = full_c[
                    c : c + 1, q * 128 : q * 128 + 128
                ]
        piece = mz.at[owner, pl.ds(r * per * nm, per * nm)]
        for d in sorted(range(1, nm), key=lambda d: abs(2 * d - nm)):
            pltpu.make_async_remote_copy(
                src_ref=piece,
                dst_ref=piece,
                send_sem=zsem.at[r, 0],
                recv_sem=zsem.at[r, 1],
                device_id={"mech": lax.rem(owner + d, nm)},
                device_id_type=MESH,
            ).start()
    def z_wait(r, which):
        others = mz.at[pl.ds(0, nm - 1), pl.ds(r * per * nm, per * nm)]
        pltpu.make_async_copy(others, others, zsem.at[r, which]).wait()

    loads[6].wait()
    loads[7].wait()
    gather_wait(m3, 2, 1, 3)
    lower = lax.broadcasted_iota(jnp.int32, (1, 128), 1) < 64
    parts = [jnp.sum(slots(m3, i), axis=0, keepdims=True) for i in range(3)]
    both = (
        jnp.where(lower, coef[0], coef[1]) * parts[0]
        + jnp.where(lower, coef[2], coef[3]) * parts[1]
        + coef[4] * parts[2]
    )
    coeffs = both[:, 0:64] + both[:, 64:128]
    mixed = jnp.sum(core[...] * coeffs, axis=1, keepdims=True)
    mixed = jnp.broadcast_to(mixed, (64, 128))
    for g in range(blocks):
        far[g : g + 1, :] = jnp.sum(
            bout[:, g * 128 : g * 128 + 128] * mixed, axis=0, keepdims=True
        )
    for r in range(4):
        z_wait(r, 1)
    a_h[...] = jnp.sum(mz[...], axis=0) + far[...]
    for c in pending:
        c.wait_send()
    gather_wait(m1, 0, 0, 3)
    gather_wait(m2, 1, 0, 3)
    gather_wait(m3, 2, 0, 3)
    for r in range(4):
        z_wait(r, 0)


def solution(mesh):
    nf = mesh.shape["flow"]
    nm = mesh.shape["mech"]

    def local(source, aperture_rest, storage, geometry, tiles, near, basis_in, core, basis_out):
        blocks, width = source.shape
        rank = core.shape[0]
        grid = (blocks, width)
        vm = pltpu.VMEM
        wide = (blocks + 16, width)
        scratch = [
            vm((6,) + wide, F32), vm(tiles.shape, F32), vm((2, width, width), F32),
            vm((blocks // 8 + 1, 2 * width, 8 * width), BF16),
            vm(near.shape, BF16), vm((rank, basis_in.shape[0]), F32), vm(core.shape, F32),
            vm((rank, basis_in.shape[0]), F32),
            vm((NV, blocks + 32, width), F32), vm((NV,) + wide, F32),
            vm(wide, F32), vm(wide, F32), vm(wide, F32), vm(wide, F32),
            vm((blocks + 8, width), F32), vm(grid, F32), vm((32, width), F32),
            vm(((nf + 2) * 8, width), F32), vm(((nf + 2) * 8, width), F32),
            vm(((nf + 1) * 8, width), F32), vm((nm,) + grid, F32),
            pltpu.SemaphoreType.DMA((8,)), pltpu.SemaphoreType.DMA((4,)),
            pltpu.SemaphoreType.DMA((4, 2)),
            pltpu.SemaphoreType.DMA((3, 2)), pltpu.SemaphoreType.DMA((4, 2)),
        ]
        anywhere = pl.BlockSpec(memory_space=pltpu.HBM)
        pressure, shift, margin = pl.pallas_call(
            functools.partial(kernel, nf, nm, blocks),
            out_shape=(
                jax.ShapeDtypeStruct(grid, F32),
                jax.ShapeDtypeStruct(grid, F32),
                jax.ShapeDtypeStruct((1, 1), F32),
            ),
            in_specs=[anywhere] * 9,
            out_specs=(
                pl.BlockSpec(memory_space=pltpu.VMEM),
                pl.BlockSpec(memory_space=pltpu.VMEM),
                pl.BlockSpec(memory_space=pltpu.SMEM),
            ),
            scratch_shapes=scratch,
            compiler_params=pltpu.CompilerParams(
                collective_id=0, has_side_effects=True, vmem_limit_bytes=63 << 20
            ),
        )(
            source, aperture_rest, storage, geometry, tiles, near,
            basis_in.T, core, basis_out.T,
        )
        end = pl.pallas_call(
            closing,
            out_shape=(jax.ShapeDtypeStruct(grid, F32), jax.ShapeDtypeStruct(grid, F32)),
            in_specs=[pl.BlockSpec(memory_space=pltpu.VMEM)] * 3,
            out_specs=(pl.BlockSpec(memory_space=pltpu.VMEM),) * 2,
        )
        return lax.cond(
            margin[0, 0] > 0.0,
            lambda: end(pressure, shift, aperture_rest),
            lambda: plain(
                source, aperture_rest, storage, geometry, tiles, near, basis_in, core, basis_out
            ),
        )

    placed = (
        P("flow", None), P("flow", None), P("flow", None), P("flow", None),
        P("flow", None, None), P("flow", None, "mech"), P("flow", None), P(), P("flow", None),
    )
    return jax.shard_map(
        local,
        mesh=mesh,
        in_specs=placed,
        out_specs=(P("flow", None), P("flow", None)),
        check_vma=False,
    )
```

```python
import functools
import jax
import jax.numpy as jnp
from jax import lax
from jax.experimental import pallas as pl
from jax.experimental.pallas import tpu as pltpu
from jax.sharding import PartitionSpec as P

F32 = jnp.float32
BF16 = jnp.bfloat16
MESH = pl.DeviceIdType.MESH
NV = 5
LEAST = 3e-3


def split(x):
    hi = x.astype(BF16)
    return hi, (x - hi.astype(F32)).astype(BF16)


CG = 5


def extended(cells, sides, width):
    for axis, dim in sides:
        count = lax.axis_size(axis)
        ends = count - 1
        head = lax.slice_in_dim(cells, 0, width, axis=dim)
        tail = lax.slice_in_dim(cells, cells.shape[dim] - width, cells.shape[dim], axis=dim)
        cells = jnp.concatenate(
            [
                lax.ppermute(tail, axis, [(i, (i + 1) % count) for i in range(ends)]),
                cells,
                lax.ppermute(head, axis, [((i + 1) % count, i) for i in range(ends)]),
            ],
            axis=dim,
        )
    return cells


def exchange_faces(v):
    return extended(v, (("flow", 0),), 1)


def operate(v, tiles, scale, storage, cond_all):
    padded = exchange_faces(v)
    local = jnp.einsum("bij,bj->bi", tiles, scale * v, precision=lax.Precision.HIGHEST) * scale
    cond = cond_all[1:]
    cprv = cond_all[:-1]
    return storage * v + local + (cond + cprv) * v - cond * padded[2:] - cprv * padded[:-2]


def squares(residual):
    return lax.psum(jnp.sum(residual * residual), "flow")


def curving(direction, image):
    return lax.psum(jnp.sum(direction * image), "flow")


def solve_flow(source, tiles, scale, storage, cond_all):
    pressure = jnp.zeros_like(source)
    residual = source
    direction = source
    norm_now = squares(residual)
    for step in range(CG):
        image = operate(direction, tiles, scale, storage, cond_all)
        alpha = norm_now / curving(direction, image)
        pressure = pressure + alpha * direction
        residual = residual - alpha * image
        norm_next = squares(residual)
        direction = residual + norm_next / norm_now * direction
        norm_now = norm_next
    return pressure


def plain(source, aperture_rest, storage, geometry, tiles, near, basis_in, core, basis_out):
    blocks, width = source.shape
    groups = lax.axis_size("mech")
    owner = lax.axis_index("mech")
    clusters = near.shape[0]
    span = near.shape[2]
    aperture = aperture_rest
    stacked = jnp.stack([aperture, geometry])
    padded = extended(stacked, (("flow", 1),), 1)
    ap_pad = padded[0]
    geo_pad = padded[1]
    cond_all = geo_pad[:-1] * (ap_pad[:-1] ** 3 + ap_pad[1:] ** 3) * 0.5
    scale = aperture**1.5
    pressure = solve_flow(source, tiles, scale, storage, cond_all)
    packed = pressure.astype(jnp.bfloat16).reshape(clusters, span * groups)
    piece = lax.dynamic_slice_in_dim(packed, owner * span, span, 1)
    partial_value = jnp.einsum(
        "cij,cj->ci", near, piece, preferred_element_type=jnp.float32
    ).reshape(blocks, width)
    coeffs = lax.psum(
        jnp.dot(pressure.reshape(-1), basis_in, precision=lax.Precision.HIGHEST), "flow"
    )
    mixed = jnp.dot(core, coeffs, precision=lax.Precision.HIGHEST)
    near_disp = lax.psum(partial_value, "mech")
    far_disp = jnp.dot(basis_out, mixed, precision=lax.Precision.HIGHEST).reshape(blocks, width)
    aperture = aperture_rest * (1.0 + 0.5 * jnp.tanh(near_disp + far_disp))
    return (pressure, aperture)


def tile_group(weights, u, g, count=8):
    hi, lo = split(u)
    left = jnp.concatenate(
        [jnp.concatenate([hi, hi], 1), jnp.concatenate([lo, jnp.zeros_like(lo)], 1)], 0
    )
    out = jnp.dot(left, weights[g, :, 0 : count * 128], preferred_element_type=F32)
    rows = [
        out[k : k + 1, k * 128 : k * 128 + 128] + out[8 + k : 9 + k, k * 128 : k * 128 + 128]
        for k in range(count)
    ]
    return jnp.concatenate(rows, axis=0)


def closing(p_in, shift, rest, p_out, a_out):
    p_out[...] = p_in[...]
    a_out[...] = rest[...] * (1.0 + 0.5 * jnp.tanh(shift[...]))


def kernel(
    nf, nm, blocks,
    src_h, ap_h, st_h, ge_h, tiles_h, near_h, bin_h, core_h, bout_h,
    p_h, a_h, f_h,
    ext, tiles, ghost, weights, near, bin_v, core, bout,
    vec, img, diag, cnext, cprev, scale, p_v, far, rows,
    m1, m2, m3, mz,
    lsem, tsem, xsem, bsem, zsem,
):
    me = lax.axis_index("flow")
    owner = lax.axis_index("mech")
    right = lax.rem(me + 1, nf)
    left = lax.rem(me + nf - 1, nf)
    head = me == 0
    tail = me == nf - 1
    groups = blocks // 8
    chunk = blocks // 4
    last = blocks - 1
    own = slice(8, 8 + blocks)
    wide = blocks + 16
    body = slice(8, 8 + wide)
    above = slice(7, 7 + wide)
    below = slice(9, 9 + wide)
    mid = slice(16, 16 + blocks)
    zero_row = jnp.zeros((1, 128), F32)

    loads = []

    def load(i, a, b):
        c = pltpu.make_async_copy(a, b, lsem.at[i])
        c.start()
        loads.append(c)

    for i, ref in enumerate((src_h, ap_h, ge_h, st_h)):
        load(i, ref, ext.at[i, pl.ds(8, blocks)])
    tloads = []
    for q in range(4):
        part = pl.ds(q * chunk, chunk)
        c = pltpu.make_async_copy(tiles_h.at[part], tiles.at[part], tsem.at[q])
        c.start()
        tloads.append(c)

    barrier = pltpu.get_barrier_semaphore()

    def greet(d, carry):
        pl.semaphore_signal(
            barrier, inc=1, device_id={"flow": lax.rem(me + d, nf)}, device_id_type=MESH
        )
        return carry

    lax.fori_loop(1, nf, greet, 0)
    for d in range(1, nm):
        pl.semaphore_signal(
            barrier, inc=1, device_id={"mech": lax.rem(owner + d, nm)}, device_id_type=MESH
        )

    def spread(buf, i, size):
        mine = buf.at[pl.ds(pl.multiple_of(me * 8, 8), size)]

        def one(d, carry):
            pltpu.make_async_remote_copy(
                src_ref=mine,
                dst_ref=mine,
                send_sem=bsem.at[i, 0],
                recv_sem=bsem.at[i, 1],
                device_id={"flow": lax.rem(me + d, nf)},
                device_id_type=MESH,
            ).start()
            return carry

        lax.fori_loop(1, nf, one, 0)

    def gather_wait(buf, i, which, size):
        others = buf.at[pl.ds(0, (nf - 1) * size)]
        pltpu.make_async_copy(others, others, bsem.at[i, which]).wait()

    def slots(buf, row):
        return buf[pl.ds(row, nf, stride=8), :]

    def spot():
        return pl.ds(pl.multiple_of(me * 8, 8), 8)

    def dot_row(i, x, y):
        rows[i : i + 1, :] = jnp.sum(x * y, axis=0, keepdims=True)

    def row_sums():
        sums = jnp.sum(rows[...].T, axis=0, keepdims=True)
        return jnp.concatenate([sums, jnp.zeros((1, 96), F32)], axis=1)

    def lane(row, i):
        return jnp.broadcast_to(row[:, i : i + 1], (1, 128))

    def total_of(x):
        x = jnp.sum(x, axis=0, keepdims=True)
        return jnp.broadcast_to(jnp.sum(x, axis=1, keepdims=True), (1, 128))

    rows[...] = jnp.zeros_like(rows)
    m1[pl.ds(nf * 8, 8), :] = jnp.zeros((8, 128), F32)
    m2[pl.ds(nf * 8, 8), :] = jnp.zeros((8, 128), F32)
    for k in range(NV):
        vec[k, 0:8, :] = jnp.zeros((8, 128), F32)
        vec[k, 8 + wide : 16 + wide, :] = jnp.zeros((8, 128), F32)
        img[k, 0:8, :] = jnp.zeros((8, 128), F32)
        img[k, 8 + blocks : wide, :] = jnp.zeros((8, 128), F32)

    for i in range(3):
        loads[i].wait()
    a = ext[1, own, :]
    b = ext[0, own, :]
    s = a * jnp.sqrt(a)
    scale[own, :] = s

    def prepare(tile, g, k):
        hi, lo = split(tile)
        weights[g, 0:128, k * 128 : k * 128 + 128] = hi
        weights[g, 128:256, k * 128 : k * 128 + 128] = lo

    for q in range(4):
        tloads[q].wait()
        for g in range(q * groups // 4, (q + 1) * groups // 4):
            for k in range(8):
                prepare(tiles[g * 8 + k], g, k)
            part = slice(8 + g * 8, 16 + g * 8)
            ext[4, part, :] = tile_group(weights, scale[part, :] * ext[0, part, :], g)

    load(4, bin_h, bin_v)
    load(5, near_h, near)
    load(6, core_h, core)
    load(7, bout_h, bout)
    loads[3].wait()
    cube = a * a * a
    half = ext[2, own, :] * 0.5
    edge = half[last:] * cube[last:]
    inner = half[:last] * (cube[:last] + cube[1:])
    cond = jnp.concatenate([inner, jnp.where(tail, edge, zero_row)], axis=0)
    cp = jnp.concatenate([zero_row, inner], axis=0)
    ahead = jnp.concatenate([b[1:], zero_row], axis=0)
    behind = jnp.concatenate([zero_row, b[:last]], axis=0)
    alone = (ext[3, own, :] + cond + cp) * b + s * ext[4, own, :] - cond * ahead - cp * behind
    img[0, own, :] = alone
    for g in (0, groups - 1):
        part = slice(8 + g * 8, 16 + g * 8)
        ext[5, part, :] = tile_group(weights, scale[part, :] * img[0, part, :], g)
    dot_row(0, b, b)
    dot_row(1, b, alone)
    dot_row(2, alone, alone)
    rows[3:4, :] = jnp.where(tail, zero_row, half[last:]) * (1.0 / 128.0)
    rows[4:5, :] = cube[last:] * (1.0 / 128.0)
    rows[5:6, :] = cube[0:1] * (1.0 / 128.0)
    m1[spot(), :] = jnp.concatenate(
        [row_sums(), b[last:], b[0:1], jnp.zeros((5, 128), F32)], axis=0
    )
    pl.semaphore_wait(barrier, nf - 1 + nm - 1)

    pending = []

    def hand_over(a, b, i, dev):
        c = pltpu.make_async_remote_copy(
            src_ref=a, dst_ref=b, send_sem=xsem.at[i, 0], recv_sem=xsem.at[i, 1],
            device_id={"flow": dev}, device_id_type=MESH,
        )
        c.start()
        pending.append(c)

    hand_over(ext.at[:, pl.ds(blocks, 8)], ext.at[:, pl.ds(0, 8)], 0, right)
    hand_over(ext.at[:, pl.ds(8, 8)], ext.at[:, pl.ds(8 + blocks, 8)], 1, left)
    spread(m1, 0, 3)
    hand_over(tiles.at[blocks - 1], ghost.at[0], 2, right)
    hand_over(tiles.at[0], ghost.at[1], 3, left)
    pending[0].wait_recv()
    pending[1].wait_recv()

    row = lax.broadcasted_iota(jnp.int32, (wide, 128), 0)
    at_tail = row == jnp.where(tail, 7 + blocks, -1)
    at_head = row == jnp.where(head, 7, -1)
    a = ext[1]
    s = a * jnp.sqrt(a)
    scale[...] = s
    cube = a * a * a
    cube_next = jnp.where(at_tail, 0.0, jnp.concatenate([cube[1:], zero_row], axis=0))
    cond = jnp.where(at_head, 0.0, ext[2] * (cube + cube_next) * 0.5)
    cp = jnp.concatenate([zero_row, cond[:-1]], axis=0)
    cnext[...] = jnp.where(at_tail, 0.0, cond)
    cprev[...] = cp
    diag[...] = ext[3] + cond + cp
    vec[0, body, :] = ext[0]
    img[0] = ext[4]

    def finish(k):
        img[k] = (
            diag[...] * vec[k, body, :]
            + scale[...] * img[k]
            - cnext[...] * vec[k, below, :]
            - cprev[...] * vec[k, above, :]
        )

    def product(k):
        for g in range(groups):
            part = slice(8 + g * 8, 16 + g * 8)
            u = scale[part, :] * vec[k, 16 + g * 8 : 24 + g * 8, :]
            img[k, part, :] = tile_group(weights, u, g)

    def ghost_product(k):
        low, high = slice(7, 8), slice(8 + blocks, 9 + blocks)
        u = jnp.concatenate(
            [
                scale[low, :] * vec[k, 15:16, :],
                scale[high, :] * vec[k, 16 + blocks : 17 + blocks, :],
                jnp.zeros((6, 128), F32),
            ],
            axis=0,
        )
        out = tile_group(weights, u, groups, 2)
        img[k, low, :] = out[0:1]
        img[k, high, :] = out[1:2]

    finish(0)
    vec[1, body, :] = img[0]
    product(1)
    pending[2].wait_recv()
    pending[3].wait_recv()
    for k in range(2):
        prepare(ghost[k], groups, k)
    ghost_product(1)
    img[1, 6:7, :] = ext[5, 6:7, :]
    img[1, 9 + blocks : 10 + blocks, :] = ext[5, 9 + blocks : 10 + blocks, :]
    finish(1)
    gather_wait(m1, 0, 1, 3)

    def following(row):
        return m1[pl.ds(8 + row, nf, stride=8), :]

    sums = slots(m1, 0)
    total = jnp.sum(sums, axis=0, keepdims=True)
    gap = slots(m1, 1) - following(2)
    flux = sums[:, 3:4] * (sums[:, 4:5] + following(0)[:, 5:6]) * gap
    bb = lane(total, 0)
    bw = lane(total, 1) + total_of(flux * gap)
    ww = lane(total, 2) + 2.0 * total_of(flux * (lane(total, 1) / bb * gap + flux))
    mean = bw / bb
    dev = jnp.sqrt(jnp.maximum(ww / bb - mean * mean, (0.01 * mean) * (0.01 * mean)))
    inv = 1.0 / dev
    shifted = (mean + 0.8 * dev) * inv
    w0 = img[0]
    b = ext[0]
    v1 = (w0 - mean * b) * inv
    w1 = (img[1] - mean * w0) * inv
    vec[1, body, :] = v1
    img[1] = w1
    vec[2, body, :] = w1 * inv - shifted * v1 - b
    pairs = {}

    def entry(j, k):
        pairs[(j, k)] = len(pairs)
        dot_row(pairs[(j, k)], vec[k, mid, :], img[j, own, :])

    def against(k):
        pairs[("g", k)] = len(pairs)
        dot_row(pairs[("g", k)], vec[k, mid, :], vec[1, mid, :])

    product(2)
    ghost_product(2)
    for j, k in ((0, 0), (0, 1), (1, 1), (0, 2), (1, 2)):
        entry(j, k)
    for k in range(3):
        against(k)
    finish(2)
    vec[3, body, :] = img[2] * inv - shifted * vec[2, body, :] - vec[1, body, :]
    product(3)
    for j, k in ((2, 2), (0, 3), (1, 3), (2, 3)):
        entry(j, k)
    against(3)
    finish(3)
    vec[4, mid, :] = (
        img[3, own, :] * inv - shifted * vec[3, mid, :] - vec[2, mid, :]
    )
    vec[4, 8:16, :] = jnp.zeros((8, 128), F32)
    vec[4, 16 + blocks : 24 + blocks, :] = jnp.zeros((8, 128), F32)
    product(4)
    for j, k in ((3, 3), (0, 4), (1, 4), (2, 4), (3, 4)):
        entry(j, k)
    against(4)
    finish(4)
    entry(4, 4)
    m2[spot(), :] = jnp.concatenate(
        [
            row_sums(),
            cnext[7 + blocks : 8 + blocks, :] * vec[4, 15 + blocks : 16 + blocks, :],
            vec[4, 16:17, :],
            jnp.zeros((5, 128), F32),
        ],
        axis=0,
    )
    spread(m2, 1, 3)
    loads[4].wait()
    loads[5].wait()
    accs = [jnp.zeros((64, 128), F32)] * NV
    for g in range(blocks):
        cut = bin_v[:, g * 128 : g * 128 + 128]
        accs = [accs[k] + cut * vec[k, 16 + g : 17 + g, :] for k in range(NV)]
    far_rows = [jnp.sum(acc.T, axis=0, keepdims=True) for acc in accs] + [zero_row[:, 0:64]]
    m3[spot(), :] = jnp.concatenate(
        [jnp.concatenate(far_rows[i : i + 2], axis=1) for i in (0, 2, 4)]
        + [jnp.zeros((5, 128), F32)],
        axis=0,
    )
    spread(m3, 2, 3)
    gather_wait(m2, 1, 1, 3)

    total = jnp.sum(slots(m2, 0), axis=0, keepdims=True)
    cross = total_of(slots(m2, 1) * m2[pl.ds(8 + 2, nf, stride=8), :])
    full = [[None] * NV for _ in range(NV)]
    for j in range(NV):
        for k in range(j, NV):
            full[j][k] = lane(total, pairs[(j, k)])
    full[4][4] = full[4][4] - 2.0 * cross
    size = [full[j][j] for j in range(NV)]
    ratio = -dev / mean
    y = [ratio * lane(total, pairs[("g", k)]) for k in range(NV)]
    low = [[None] * NV for _ in range(NV)]
    pivot = [None] * NV
    least = None
    for j in range(NV):
        pivot[j] = 1.0 / full[j][j]
        margin = full[j][j] - LEAST * size[j]
        least = margin if j == 0 else jnp.minimum(least, margin)
        for i in range(j + 1, NV):
            low[i][j] = full[j][i] * pivot[j]
        for i in range(j + 1, NV):
            for k in range(i, NV):
                full[i][k] = full[i][k] - low[i][j] * full[j][k]
            y[i] = y[i] - low[i][j] * y[j]
    coef = [y[j] * pivot[j] for j in range(NV)]
    for j in range(NV - 2, -1, -1):
        for i in range(j + 1, NV):
            coef[j] = coef[j] - low[i][j] * coef[i]
    coef[0] = coef[0] + 1.0 / mean
    p = coef[0] * vec[0, mid, :]
    for k in range(1, NV):
        p = p + coef[k] * vec[k, mid, :]
    p_v[0:blocks, :] = p
    f_h[0, 0] = least[0, 0]
    p_h[...] = p

    clusters = blocks // nm
    mine = jnp.zeros((clusters, 128), F32)
    for q in range(nm):
        mine = jnp.where(owner == q, p_v[pl.ds(q, clusters, stride=nm), :], mine)
    mine = mine.astype(BF16)
    per = clusters // 2
    for r in range(2):
        for c in range(r * per, (r + 1) * per):
            full_c = lax.dot_general(
                mine, near[c], (((1,), (1,)), ((), ())), preferred_element_type=F32
            )
            for q in range(nm):
                mz[owner, nm * c + q : nm * c + q + 1, :] = full_c[
                    c : c + 1, q * 128 : q * 128 + 128
                ]
        piece = mz.at[owner, pl.ds(r * per * nm, per * nm)]
        for d in sorted(range(1, nm), key=lambda d: abs(2 * d - nm)):
            pltpu.make_async_remote_copy(
                src_ref=piece,
                dst_ref=piece,
                send_sem=zsem.at[r, 0],
                recv_sem=zsem.at[r, 1],
                device_id={"mech": lax.rem(owner + d, nm)},
                device_id_type=MESH,
            ).start()
    def z_wait(r, which):
        others = mz.at[pl.ds(0, nm - 1), pl.ds(r * per * nm, per * nm)]
        pltpu.make_async_copy(others, others, zsem.at[r, which]).wait()

    loads[6].wait()
    loads[7].wait()
    gather_wait(m3, 2, 1, 3)
    lower = lax.broadcasted_iota(jnp.int32, (1, 128), 1) < 64
    parts = [jnp.sum(slots(m3, i), axis=0, keepdims=True) for i in range(3)]
    both = (
        jnp.where(lower, coef[0], coef[1]) * parts[0]
        + jnp.where(lower, coef[2], coef[3]) * parts[1]
        + coef[4] * parts[2]
    )
    coeffs = both[:, 0:64] + both[:, 64:128]
    mixed = jnp.sum(core[...] * coeffs, axis=1, keepdims=True)
    mixed = jnp.broadcast_to(mixed, (64, 128))
    for g in range(blocks):
        far[g : g + 1, :] = jnp.sum(
            bout[:, g * 128 : g * 128 + 128] * mixed, axis=0, keepdims=True
        )
    for r in range(2):
        z_wait(r, 1)
    a_h[...] = jnp.sum(mz[...], axis=0) + far[...]
    for c in pending:
        c.wait_send()
    gather_wait(m1, 0, 0, 3)
    gather_wait(m2, 1, 0, 3)
    gather_wait(m3, 2, 0, 3)
    for r in range(2):
        z_wait(r, 0)


def solution(mesh):
    nf = mesh.shape["flow"]
    nm = mesh.shape["mech"]

    def local(source, aperture_rest, storage, geometry, tiles, near, basis_in, core, basis_out):
        blocks, width = source.shape
        rank = core.shape[0]
        grid = (blocks, width)
        vm = pltpu.VMEM
        wide = (blocks + 16, width)
        scratch = [
            vm((6,) + wide, F32), vm(tiles.shape, F32), vm((2, width, width), F32),
            vm((blocks // 8 + 1, 2 * width, 8 * width), BF16),
            vm(near.shape, BF16), vm((rank, basis_in.shape[0]), F32), vm(core.shape, F32),
            vm((rank, basis_in.shape[0]), F32),
            vm((NV, blocks + 32, width), F32), vm((NV,) + wide, F32),
            vm(wide, F32), vm(wide, F32), vm(wide, F32), vm(wide, F32),
            vm((blocks + 8, width), F32), vm(grid, F32), vm((32, width), F32),
            vm(((nf + 2) * 8, width), F32), vm(((nf + 2) * 8, width), F32),
            vm(((nf + 1) * 8, width), F32), vm((nm,) + grid, F32),
            pltpu.SemaphoreType.DMA((8,)), pltpu.SemaphoreType.DMA((4,)),
            pltpu.SemaphoreType.DMA((4, 2)),
            pltpu.SemaphoreType.DMA((3, 2)), pltpu.SemaphoreType.DMA((4, 2)),
        ]
        anywhere = pl.BlockSpec(memory_space=pltpu.HBM)
        pressure, shift, margin = pl.pallas_call(
            functools.partial(kernel, nf, nm, blocks),
            out_shape=(
                jax.ShapeDtypeStruct(grid, F32),
                jax.ShapeDtypeStruct(grid, F32),
                jax.ShapeDtypeStruct((1, 1), F32),
            ),
            in_specs=[anywhere] * 9,
            out_specs=(
                pl.BlockSpec(memory_space=pltpu.VMEM),
                pl.BlockSpec(memory_space=pltpu.VMEM),
                pl.BlockSpec(memory_space=pltpu.SMEM),
            ),
            scratch_shapes=scratch,
            compiler_params=pltpu.CompilerParams(
                collective_id=0, has_side_effects=True, vmem_limit_bytes=63 << 20
            ),
        )(
            source, aperture_rest, storage, geometry, tiles, near,
            basis_in.T, core, basis_out.T,
        )
        end = pl.pallas_call(
            closing,
            out_shape=(jax.ShapeDtypeStruct(grid, F32), jax.ShapeDtypeStruct(grid, F32)),
            in_specs=[pl.BlockSpec(memory_space=pltpu.VMEM)] * 3,
            out_specs=(pl.BlockSpec(memory_space=pltpu.VMEM),) * 2,
        )
        return lax.cond(
            margin[0, 0] > 0.0,
            lambda: end(pressure, shift, aperture_rest),
            lambda: plain(
                source, aperture_rest, storage, geometry, tiles, near, basis_in, core, basis_out
            ),
        )

    placed = (
        P("flow", None), P("flow", None), P("flow", None), P("flow", None),
        P("flow", None, None), P("flow", None, "mech"), P("flow", None), P(), P("flow", None),
    )
    return jax.shard_map(
        local,
        mesh=mesh,
        in_specs=placed,
        out_specs=(P("flow", None), P("flow", None)),
        check_vma=False,
    )
```
